32 devices in a mesh: groups: 2 (over y), row: 4 (over z), col: 2 (over x), pole: 2 (over core).
Axes of the slice: x: 2, y: 2, z: 4, core: 2. Of those that a mesh axis runs over, the one named last changes fastest.
Arguments:
- inverse: bfloat16 [4, 2, 8192, 8192], P(('groups', 'pole'), None, 'row', 'col'), parts along dimension 0, may hold values from -6 to 6
- lower: bfloat16 [4, 8192, 2, 3, 256], P(('groups', 'pole'), ('col', 'row')), parts along dimension 0, may hold values from -0.0625 to 0.0625
- upper: bfloat16 [4, 8192, 2, 3, 256], P(('groups', 'pole'), ('row', 'col')), parts along dimension 0, may hold values from -0.0625 to 0.0625
- diag_inverse: bfloat16 [4, 3, 2, 256, 256], P(('groups', 'pole')), parts along dimension 0, may hold values from -6 to 6
- weights: float32 [4, 2], P(('groups', 'pole')), parts along dimension 0, may hold values from -4 to 4
- pattern: int32 [6, 16], P('groups'), parts along dimension 0, may hold values from 0 to 31, as said below
Outputs:
- column_density: float32 [16384, 3, 256], P(('groups', 'row', 'col', 'pole')), parts along dimension 0
- row_density: float32 [16384, 3, 256], P(('groups', 'col', 'row', 'pole')), parts along dimension 0
- diagonal_density: float32 [6, 256, 256], P('groups'), parts along dimension 0
The draws below stay inside these ranges and needn't reach their ends.
There are 2 independent parts, one for each index of `groups`. The reference program is written for one: setup_inputs(seed, part) draws one part's arguments, and reference() takes and returns one part's arrays. A program takes and returns all parts, laid end to end along the dimension named above; each array names one. Nothing has to cross between parts.
Inputs may be any that keep to these rules, and one draw needn't show every extreme that they name: `pattern`: each row names 16 different ancestor blocks, and the rows together name every ancestor block.
All inputs are finite; a program needn't handle non-finite values.
Results may differ from the reference program's by a relative error of at most 0.0003.
Values may be sent and summed in bfloat16 or wider, within the bound.
No kernel may reach another device: no remote copies, remote signals or barrier semaphores. Data moves between devices by JAX's collectives and lax.ppermute only.
A program may use at most 192 MiB of HBM per device.

```python
import jax
import jax.numpy as jnp
from jax import lax

BW = 256
NB = 32
PAT = 16
SUPER = 3
ANC = 8192
POLES = 2


def draw_pattern(key, part):
    order = jax.random.permutation(jax.random.fold_in(key, 17), NB).astype(jnp.int32)
    supers = jnp.arange(SUPER, dtype=jnp.int32)[:, None]
    slots = jnp.arange(PAT, dtype=jnp.int32)[None, :]
    positions = (supers * PAT + slots) % NB
    return order[positions].astype(jnp.int32)


def levels(key, dims, shards, least, high):
    def one(axis_at, blocks):
        heights = jax.random.uniform(jax.random.fold_in(jax.random.fold_in(key, 6), axis_at), (blocks,), jnp.float32, least / len(shards), high / len(shards))
        return jnp.repeat(jnp.exp(heights), dims[axis_at] // blocks).reshape((-1,) + (1,) * (len(dims) - axis_at - 1))

    factor_of = one(*shards[0])
    for cut in shards[1:]:
        factor_of = factor_of * one(*cut)
    return factor_of


def normal_values(own_key, dims, deviation, most, split=(), kind=jnp.bfloat16):
    array = deviation * jax.random.normal(own_key, dims, jnp.float32)
    if split:
        array = array * levels(own_key, dims, split, -0.22, 0.18)
    return jnp.clip(array, -most, most).astype(kind)


def setup_inputs(seed: int = 0, part: int = 0) -> dict:
    splits = jax.random.split(jax.random.key(seed), 7)
    own_keys = jax.random.split(jax.random.fold_in(splits[6], part), 7)
    inverse = normal_values(own_keys[0], (POLES, 2, ANC, ANC), 1.0, 6.0, ((0, 2), (2, 4), (3, 2)))
    lower = normal_values(own_keys[1], (POLES, ANC, 2, SUPER, BW), (2 * PAT * BW) ** -0.5, 0.0625, ((0, 2), (1, 8)))
    upper = normal_values(own_keys[2], (POLES, ANC, 2, SUPER, BW), (2 * PAT * BW) ** -0.5, 0.0625, ((0, 2), (1, 8)))
    diag_inverse = normal_values(own_keys[3], (POLES, SUPER, 2, BW, BW), 1.0, 6.0, ((0, 2),))
    weights = normal_values(own_keys[4], (POLES, 2), 1.0, 4.0, ((0, 2),), jnp.float32)
    pattern = draw_pattern(jax.random.fold_in(jax.random.fold_in(splits[6], part), 71), part)
    return dict(inverse=inverse, lower=lower, upper=upper, diag_inverse=diag_inverse, weights=weights, pattern=pattern)


def kept_rows(pattern):
    blocks = jnp.arange(ANC, dtype=jnp.int32) // BW
    hits = pattern[:, :, None] == blocks[None, None, :]
    return jnp.any(hits, axis=1)


def transposed_dot(left, right):
    return lax.dot_general(left, right, (((0,), (0,)), ((), ())), preferred_element_type=jnp.float32)


def reference(inverse, lower, upper, diag_inverse, weights, pattern):
    keep = jnp.transpose(kept_rows(pattern))[:, None, :, None]
    column_density = jnp.zeros((ANC, SUPER * BW), jnp.float32)
    row_density = jnp.zeros((ANC, SUPER * BW), jnp.float32)
    diagonal_density = jnp.zeros((SUPER, BW, BW), jnp.float32)
    highest = lax.Precision.HIGHEST
    for pole in range(POLES):
        real_inverse = inverse[pole, 0]
        imag_inverse = inverse[pole, 1]
        lower_kept = jnp.where(keep, lower[pole], jnp.zeros_like(lower[pole]))
        upper_kept = jnp.where(keep, upper[pole], jnp.zeros_like(upper[pole]))
        real_lower = lower_kept[:, 0].reshape(ANC, SUPER * BW)
        imag_lower = lower_kept[:, 1].reshape(ANC, SUPER * BW)
        real_upper = upper_kept[:, 0].reshape(ANC, SUPER * BW)
        imag_upper = upper_kept[:, 1].reshape(ANC, SUPER * BW)
        column_real = -(jnp.dot(real_inverse, real_lower, preferred_element_type=jnp.float32)
                        - jnp.dot(imag_inverse, imag_lower, preferred_element_type=jnp.float32))
        column_imag = -(jnp.dot(real_inverse, imag_lower, preferred_element_type=jnp.float32)
                        + jnp.dot(imag_inverse, real_lower, preferred_element_type=jnp.float32))
        row_real = -(transposed_dot(real_inverse, real_upper) - transposed_dot(imag_inverse, imag_upper))
        row_imag = -(transposed_dot(real_inverse, imag_upper) + transposed_dot(imag_inverse, real_upper))
        weight_real = weights[pole, 0]
        weight_imag = weights[pole, 1]
        column_density = column_density + weight_real * column_imag + weight_imag * column_real
        row_density = row_density + weight_real * row_imag + weight_imag * row_real
        zeta_real = row_real.reshape(ANC, SUPER, BW)
        zeta_imag = row_imag.reshape(ANC, SUPER, BW)
        lower_real = real_lower.astype(jnp.float32).reshape(ANC, SUPER, BW)
        lower_imag = imag_lower.astype(jnp.float32).reshape(ANC, SUPER, BW)
        prod_real = (jnp.einsum("nsa,nsb->sab", zeta_real, lower_real, precision=highest)
                     - jnp.einsum("nsa,nsb->sab", zeta_imag, lower_imag, precision=highest))
        prod_imag = (jnp.einsum("nsa,nsb->sab", zeta_real, lower_imag, precision=highest)
                     + jnp.einsum("nsa,nsb->sab", zeta_imag, lower_real, precision=highest))
        given = diag_inverse[pole].astype(jnp.float32)
        diag_real = given[:, 0] - prod_real
        diag_imag = given[:, 1] - prod_imag
        diagonal_density = diagonal_density + weight_real * diag_imag + weight_imag * diag_real
    return (column_density.reshape(ANC, SUPER, BW), row_density.reshape(ANC, SUPER, BW), diagonal_density)
```

```python
import functools

import jax
import jax.numpy as jnp
from jax import lax
from jax.experimental import pallas as pl
from jax.experimental.pallas import tpu as pltpu
from jax.sharding import PartitionSpec as P

VMEM_LIMIT = 56 * 1024 * 1024
F32 = jnp.float32
BF16 = jnp.bfloat16


def params(**kw):
    return pltpu.CompilerParams(vmem_limit_bytes=VMEM_LIMIT, **kw)


def cost(flops, nbytes):
    return pl.CostEstimate(flops=int(flops), bytes_accessed=int(nbytes), transcendentals=0)


def whole_vmem():
    return pl.BlockSpec(memory_space=pltpu.VMEM)


def smem():
    return pl.BlockSpec(memory_space=pltpu.SMEM)


def unit_tables(pattern, shards, units, unit_rows, width):
    supers = pattern.shape[0]
    block = (lax.iota(jnp.int32, shards * units) * unit_rows) // width
    hits = jnp.any(pattern[:, :, None] == block[None, None, :], axis=1)
    flags = jnp.transpose(hits).reshape(shards, units * supers).astype(jnp.int32)
    places = lax.iota(jnp.int32, units * supers)
    before = (places[:, None] < places[None, :]).astype(jnp.int32)
    rank = jnp.sum(flags[:, :, None] * before[None], axis=1)
    slot = jnp.where(flags > 0, rank, -1)
    most = jnp.max(jnp.sum(flags, axis=1))
    return slot, most


def pack_kernel(units, supers, unit_rows, transposed, slot_ref, x_ref, *out_refs):
    for u in range(units):
        for s in range(supers):
            slot = slot_ref[u * supers + s]
            for piece in range(supers):

                @pl.when(jnp.logical_and(slot >= piece * units, slot < (piece + 1) * units))
                def _():
                    at = slot - piece * units
                    for h in range(2):
                        tile = x_ref[h, s, u * unit_rows : (u + 1) * unit_rows, :]
                        out_refs[piece][at, h] = tile.T if transposed else tile


def pack(x, slot, units, unit_rows, transposed):
    supers, width = x.shape[1], x.shape[3]
    shape = (units, 2, width, unit_rows) if transposed else (units, 2, unit_rows, width)
    return pl.pallas_call(
        functools.partial(pack_kernel, units, supers, unit_rows, transposed),
        out_shape=[jax.ShapeDtypeStruct(shape, x.dtype)] * supers,
        in_specs=[smem(), whole_vmem()],
        out_specs=[whole_vmem()] * supers,
        compiler_params=params(),
        cost_estimate=cost(0, 4 * x.size),
        name="pack",
    )(slot, x)


def line_gather(x, axis, n):
    hops = []
    right = left = x
    for t in range(1, n):
        right = lax.ppermute(right, axis, [(i, i + 1) for i in range(t - 1, n - 1)])
        left = lax.ppermute(left, axis, [(i + 1, i) for i in range(0, n - t)])
        hops.append((right, left))
    return hops


def pick(shards, d):
    return lax.dynamic_index_in_dim(shards, d, 0, keepdims=False)


def line_scatter(shards, axis, n):
    i = lax.axis_index(axis)
    if n == 1:
        return shards[0]
    if n == 2:
        return pick(shards, i) + lax.ppermute(pick(shards, 1 - i), axis, [(0, 1), (1, 0)])
    right = left = None
    for t in range(n - 1):
        send_right = pick(shards, jnp.clip(n - 1 - t + i, 0, n - 1))
        send_left = pick(shards, jnp.clip(t - (n - 1 - i), 0, n - 1))
        if t:
            send_right, send_left = send_right + right, send_left + left
        right = lax.ppermute(send_right, axis, [(j, j + 1) for j in range(t + 1)])
        left = lax.ppermute(send_left, axis, [(n - 1 - j, n - 2 - j) for j in range(t + 1)])
    return pick(shards, i) + right + left


def direct_sum(x, axes, n):
    i = lax.axis_index(axes)
    parts = x.reshape((n, -1) + x.shape[1:])
    total = pick(parts, i)
    for k in range(1, n):
        ring = [(j, (j + k) % n) for j in range(n)]
        total = total + lax.ppermute(pick(parts, (i + k) % n), axes, ring)
    gathered = [total]
    for k in range(1, n):
        gathered.append(lax.ppermute(total, axes, [((j + k) % n, j) for j in range(n)]))
    stacked = jnp.concatenate([jnp.stack(gathered)] * 2)
    return lax.dynamic_slice_in_dim(stacked, (n - i) % n, n, 0).reshape(x.shape)


def row_kernel(units, supers, sources, width, unit_rows, slot_ref, weight_ref, a_ref, *refs):
    piece_refs = refs[: sources * supers]
    out_ref, left, acc = refs[sources * supers :]
    half = width
    acc[...] = jnp.zeros_like(acc)

    def one(unit, _):
        source = unit // units
        for s in range(supers):
            slot = slot_ref[unit * supers + s]
            for q in range(sources):
                for piece in range(supers):

                    @pl.when(
                        jnp.logical_and(
                            source == q, jnp.logical_and(slot >= piece * units, slot < (piece + 1) * units)
                        )
                    )
                    def _():
                        at = slot - piece * units
                        real = piece_refs[q * supers + piece][at, 0]
                        imag = piece_refs[q * supers + piece][at, 1]
                        left[:half, :unit_rows] = real
                        left[:half, unit_rows:] = -imag
                        left[half:, :unit_rows] = imag
                        left[half:, unit_rows:] = real

            @pl.when(slot >= 0)
            def _():
                rows = pl.ds(pl.multiple_of(unit * unit_rows, unit_rows), unit_rows)
                acc[s] += jnp.dot(left[:, :unit_rows], a_ref[0, rows, :], preferred_element_type=F32) + jnp.dot(
                    left[:, unit_rows:], a_ref[1, rows, :], preferred_element_type=F32
                )

        return 0

    lax.fori_loop(0, sources * units, one, 0)
    for s in range(supers):
        out_ref[0, s * width : (s + 1) * width, :] = -(
            weight_ref[1] * acc[s, :half, :] + weight_ref[0] * acc[s, half:, :]
        )


def row_product(inverse, slot, weights, pieces, units, unit_rows, width, tile):
    supers = len(pieces[0])
    sources = len(pieces)
    part_rows, part_cols = inverse.shape[1:]
    flat = [p for group in pieces for p in group]
    return pl.pallas_call(
        functools.partial(row_kernel, units, supers, sources, width, unit_rows),
        out_shape=jax.ShapeDtypeStruct((part_cols // tile, supers * width, tile), F32),
        grid=(part_cols // tile,),
        in_specs=[smem(), smem(), pl.BlockSpec((2, part_rows, tile), lambda j: (0, 0, j))] + [whole_vmem()] * len(flat),
        out_specs=pl.BlockSpec((1, supers * width, tile), lambda j: (j, 0, 0)),
        scratch_shapes=[pltpu.VMEM((2 * width, 2 * unit_rows), BF16), pltpu.VMEM((supers, 2 * width, tile), F32)],
        compiler_params=params(),
        cost_estimate=cost(4 * supers * part_rows * part_cols * width, 4 * part_rows * part_cols),
        name="row_product",
    )(slot, weights, inverse, *flat)


def column_kernel(cfg, source_ref, slot_ref, *refs):
    units, supers, sources, width, unit_rows, part_rows, first, last, u_sources = cfg
    refs = list(refs)
    weight_ref = refs.pop(0)
    acc_in = None if first else refs.pop(0)
    a_ref = refs.pop(0)
    pieces = [refs.pop(0) for _ in range(sources * supers)]
    u_pieces = [refs.pop(0) for _ in range(u_sources * supers)] if last else []
    if last:
        x_ref, t_ref, acc = refs.pop(0), refs.pop(0), None
    else:
        acc = refs.pop(0)
    right = refs.pop(0)
    if last:
        acc = refs.pop(0)
    step = pl.program_id(0)
    if first:

        @pl.when(step == 0)
        def _():
            acc[...] = jnp.zeros_like(acc)
    else:
        sem = refs.pop(0)

        @pl.when(step == 0)
        def _():
            copy = pltpu.make_async_copy(acc_in, acc, sem)
            copy.start()
            copy.wait()

    source = step // units
    shard = source_ref[source]
    place = shard * units + step % units
    rows_step = min(512, part_rows)

    for s in range(supers):
        slot = jnp.where(shard >= 0, slot_ref[jnp.maximum(place, 0) * supers + s], -1)
        for q in range(sources):
            for piece in range(supers):

                @pl.when(
                    jnp.logical_and(source == q, jnp.logical_and(slot >= piece * units, slot < (piece + 1) * units))
                )
                def _():
                    at = slot - piece * units
                    real = pieces[q * supers + piece][at, 0]
                    imag = pieces[q * supers + piece][at, 1]
                    right[:unit_rows, :width] = real
                    right[:unit_rows, width:] = imag
                    right[unit_rows:, :width] = -imag
                    right[unit_rows:, width:] = real

        @pl.when(slot >= 0)
        def _():
            def tile(m, _):
                rows = pl.ds(pl.multiple_of(m * rows_step, rows_step), rows_step)
                acc[s, rows, :] += jnp.dot(
                    a_ref[0, rows, :], right[:unit_rows, :], preferred_element_type=F32
                ) + jnp.dot(a_ref[1, rows, :], right[unit_rows:, :], preferred_element_type=F32)
                return 0

            lax.fori_loop(0, part_rows // rows_step, tile, 0)

    if last:

        @pl.when(step == sources * units - 1)
        def _():
            weight_real = weight_ref[0]
            weight_imag = weight_ref[1]
            t_ref[...] = jnp.zeros_like(t_ref)

            def chunk(k, _):
                rows = pl.ds(pl.multiple_of(k * unit_rows, unit_rows), unit_rows)
                for s in range(supers):
                    first_acc = acc[s, rows, :width]
                    second_acc = acc[s, rows, width:]
                    mix = weight_imag * first_acc + weight_real * second_acc
                    x_ref[rows, s * width : (s + 1) * width] = -mix
                    slot = slot_ref[slot_base(k) * supers + s]

                    @pl.when(slot >= 0)
                    def _():
                        other = weight_real * first_acc - weight_imag * second_acc
                        stacked = jnp.concatenate([mix, other], axis=0)
                        high = stacked.astype(BF16)
                        low = (stacked - high.astype(F32)).astype(BF16)
                        for q in range(u_sources):
                            for piece in range(supers):

                                @pl.when(
                                    jnp.logical_and(
                                        k // units == q,
                                        jnp.logical_and(slot >= piece * units, slot < (piece + 1) * units),
                                    )
                                )
                                def _():
                                    at = slot - piece * units
                                    real = u_pieces[q * supers + piece][at, 0]
                                    imag = u_pieces[q * supers + piece][at, 1]
                                    both = jnp.concatenate([real, imag], axis=1)
                                    t_ref[s] += jnp.dot(both, high, preferred_element_type=F32) + jnp.dot(
                                        both, low, preferred_element_type=F32
                                    )

                return 0

            def slot_base(k):
                return source_ref[sources] * units + k

            lax.fori_loop(0, part_rows // unit_rows, chunk, 0)


def column_phase(inverse, acc, sources, col_base, u_base, slot, weights, pieces, u_pieces, units, unit_rows, width):
    first = acc is None
    last = u_pieces is not None
    supers = len(pieces[0])
    n_source = len(pieces)
    part_rows, part_cols = inverse.shape[1:]
    u_sources = len(u_pieces) if last else 0
    flat = [p for group in pieces for p in group]
    u_flat = [p for group in u_pieces for p in group] if last else []
    shards = jnp.where(sources >= 0, col_base + sources, -1)
    prefetch = jnp.concatenate([shards, u_base[None], sources]).astype(jnp.int32)
    cfg = (units, supers, n_source, width, unit_rows, part_rows, first, last, u_sources)

    def a_map(g, src, _):
        return (0, 0, jnp.maximum(src[n_source + 1 + g // units], 0) * units + g % units)

    acc_shape = (supers, part_rows, 2 * width)
    in_specs = [smem()] + ([] if first else [pl.BlockSpec(memory_space=pl.ANY)])
    in_specs += [pl.BlockSpec((2, part_rows, unit_rows), a_map)]
    in_specs += [whole_vmem()] * (len(flat) + len(u_flat))
    scratch = [pltpu.VMEM((2 * unit_rows, 2 * width), BF16)]
    if last:
        out_shape = [
            jax.ShapeDtypeStruct((part_rows, supers * width), F32),
            jax.ShapeDtypeStruct((supers, width, width), F32),
        ]
        out_specs = [whole_vmem(), whole_vmem()]
        scratch.append(pltpu.VMEM(acc_shape, F32))
    else:
        out_shape = jax.ShapeDtypeStruct(acc_shape, F32)
        out_specs = whole_vmem()
    if not first:
        scratch.append(pltpu.SemaphoreType.DMA)
    return pl.pallas_call(
        functools.partial(column_kernel, cfg),
        out_shape=out_shape,
        grid_spec=pltpu.PrefetchScalarGridSpec(
            num_scalar_prefetch=2,
            grid=(n_source * units,),
            in_specs=in_specs,
            out_specs=out_specs,
            scratch_shapes=scratch,
        ),
        compiler_params=params(),
        cost_estimate=cost(
            4 * supers * part_rows * units * n_source * unit_rows * width, 4 * part_rows * units * n_source * unit_rows
        ),
        name="column_phase",
    )(prefetch, slot, weights, *([] if first else [acc]), inverse, *flat, *u_flat)


def body(inverse, lower, upper, diag_inverse, weights, pattern):
    n_group = lax.axis_size("groups")
    n_row = lax.axis_size("row")
    n_col = lax.axis_size("col")
    n_pole = lax.axis_size("pole")
    row_index = lax.axis_index("row")
    col_index = lax.axis_index("col")
    local_rows, _, supers, width = lower.shape[1:]
    inverse = inverse[0]
    part_rows, part_cols = inverse.shape[1:]
    unit_rows = min(width, local_rows)
    units = local_rows // unit_rows
    weight = weights[0]

    slot, most = unit_tables(pattern, n_row * n_col, units, unit_rows, width)
    most = most.astype(F32)
    for k in range(1, n_group):
        most = jnp.maximum(most, lax.ppermute(most, "groups", [(j, (j + k) % n_group) for j in range(n_group)]))
    crowded = most > (supers - 1) * units
    flat_slot = slot.reshape(-1)

    lower_parts = jnp.transpose(lower[0], (1, 2, 0, 3))
    own_lower = pack(lower_parts, pick(slot, col_index * n_row + row_index), units, unit_rows, False)
    upper_parts = jnp.transpose(upper[0], (1, 2, 0, 3))
    own_upper = pack(upper_parts, pick(slot, row_index * n_col + col_index), units, unit_rows, True)

    def gather(pieces, axis, n):
        hops = [line_gather(p, axis, n) for p in pieces[:-1]]

        def send(x):
            return line_gather(x, axis, n)

        def skip(x):
            return [(jnp.zeros_like(x), jnp.zeros_like(x)) for _ in range(1, n)]

        hops.append(lax.cond(crowded, send, skip, pieces[-1]))
        return [[[h[t][side] for h in hops] for side in range(2)] for t in range(n - 1)]

    lower_hops = gather(own_lower, "row", n_row)
    upper_hops = gather(own_upper, "col", n_col)

    by_col = []
    for q in range(n_col):
        chosen = own_upper
        for t in range(1, n_col):
            chosen = [
                jnp.where(col_index - t == q, left, jnp.where(col_index + t == q, right, now))
                for now, left, right in zip(chosen, upper_hops[t - 1][0], upper_hops[t - 1][1])
            ]
        by_col.append(chosen)

    upper_base = row_index * n_col
    lower_base = col_index * n_row
    acc = column_phase(
        inverse, None, row_index[None], lower_base, upper_base, flat_slot, weight, [own_lower], None, units, unit_rows, width
    )

    tile = min(512, part_cols)
    row_slot = lax.dynamic_slice_in_dim(slot, upper_base, n_col, 0).reshape(-1)
    row_tiles = row_product(inverse, row_slot, weight, by_col, units, unit_rows, width, tile)

    for t in range(1, n_row):
        low = jnp.where(row_index - t >= 0, row_index - t, -1)
        high = jnp.where(row_index + t < n_row, row_index + t, -1)
        done = t == n_row - 1
        acc = column_phase(
            inverse, acc, jnp.stack([low, high]), lower_base, upper_base, flat_slot, weight, lower_hops[t - 1],
            by_col if done else None, units, unit_rows, width,
        )
    x_part, t_part = acc

    share = part_cols // (n_row * n_pole)
    if share != tile:
        row_tiles = jnp.transpose(row_tiles, (1, 0, 2)).reshape(supers * width, n_row * n_pole, share)
        row_tiles = jnp.transpose(row_tiles, (1, 0, 2))
    row_tiles = row_tiles.reshape(n_row, n_pole, supers * width, share)
    row_sum = line_scatter(jnp.swapaxes(row_tiles, 0, 1), "pole", n_pole)
    row_sum = line_scatter(row_sum, "row", n_row)
    row_density = jnp.transpose(row_sum).reshape(share, supers, width)

    share = part_rows // (n_col * n_pole)
    x_part = jnp.swapaxes(x_part.reshape(n_col, n_pole, share, supers * width), 0, 1)
    col_sum = line_scatter(x_part, "pole", n_pole)
    col_sum = line_scatter(col_sum, "col", n_col)
    column_density = col_sum.reshape(share, supers, width)

    given = diag_inverse[0].astype(F32)
    own_term = weight[0] * given[:, 1] + weight[1] * given[:, 0]
    owner = jnp.logical_and(row_index == 0, col_index == 0)
    t_part = (t_part + jnp.where(owner, own_term, 0.0)).reshape(n_pole, -1, width)
    t_sum = line_scatter(t_part, "pole", n_pole)
    t_sum = direct_sum(t_sum, ("row", "col"), n_row * n_col)
    others = line_gather(t_sum, "pole", n_pole)
    pole_index = lax.axis_index("pole")
    whole = []
    for q in range(n_pole):
        chosen = t_sum
        for t in range(1, n_pole):
            chosen = jnp.where(
                pole_index - t == q, others[t - 1][0], jnp.where(pole_index + t == q, others[t - 1][1], chosen)
            )
        whole.append(chosen)
    diagonal_density = jnp.stack(whole).reshape(supers, width, width)
    return (column_density, row_density, diagonal_density)


def solution(mesh):
    return jax.shard_map(
        body,
        mesh=mesh,
        in_specs=(
            P(("groups", "pole"), None, "row", "col"),
            P(("groups", "pole"), ("col", "row"), None, None, None),
            P(("groups", "pole"), ("row", "col"), None, None, None),
            P(("groups", "pole"), None, None, None, None),
            P(("groups", "pole"), None),
            P("groups", None),
        ),
        out_specs=(
            P(("groups", "row", "col", "pole"), None, None),
            P(("groups", "col", "row", "pole"), None, None),
            P("groups", None, None),
        ),
        check_vma=False,
    )
```

```python
import functools

import jax
import jax.numpy as jnp
from jax import lax
from jax.experimental import pallas as pl
from jax.experimental.pallas import tpu as pltpu
from jax.sharding import PartitionSpec as P

VMEM_LIMIT = 56 * 1024 * 1024
F32 = jnp.float32
BF16 = jnp.bfloat16


def params(limit=VMEM_LIMIT, **kw):
    return pltpu.CompilerParams(vmem_limit_bytes=limit, **kw)


def cost(flops, nbytes):
    return pl.CostEstimate(flops=int(flops), bytes_accessed=int(nbytes), transcendentals=0)


def fence(tree):
    return lax.optimization_barrier(tree)


def whole_vmem():
    return pl.BlockSpec(memory_space=pltpu.VMEM)


def smem():
    return pl.BlockSpec(memory_space=pltpu.SMEM)


def unit_tables(pattern, shards, units, unit_rows, width):
    supers = pattern.shape[0]
    block = (lax.iota(jnp.int32, shards * units) * unit_rows) // width
    hits = jnp.any(pattern[:, :, None] == block[None, None, :], axis=1)
    flags = jnp.transpose(hits).reshape(shards, units * supers).astype(jnp.int32)
    places = lax.iota(jnp.int32, units * supers)
    before = (places[:, None] < places[None, :]).astype(jnp.int32)
    rank = jnp.sum(flags[:, :, None] * before[None], axis=1)
    slot = jnp.where(flags > 0, rank, -1)
    most = jnp.max(jnp.sum(flags, axis=1))
    return slot, most


class Sizes:
    def __init__(self, units, supers, unit_rows, width):
        self.units, self.supers, self.unit_rows, self.width = units, supers, unit_rows, width
        self.main = units * max(supers - 1, 1)
        self.spare = units * supers - self.main

    def usual(self):
        size = Sizes(self.units, self.supers, self.unit_rows, self.width)
        size.spare = 0
        return size


def any_space():
    return pl.BlockSpec(memory_space=pl.ANY)


def pack_kernel(size, transposed, slot_ref, x_ref, main_ref, spare_ref):
    rows = size.unit_rows
    for u in range(size.units):
        for s in range(size.supers):
            slot = slot_ref[u * size.supers + s]

            def store(ref, at):
                for h in range(2):
                    tile = x_ref[h, s, u * rows : (u + 1) * rows, :]
                    ref[at, h] = tile.T if transposed else tile

            @pl.when(jnp.logical_and(slot >= 0, slot < size.main))
            def _():
                store(main_ref, slot)

            if size.spare:

                @pl.when(slot >= size.main)
                def _():
                    store(spare_ref, slot - size.main)


def pack(x, slot, size, transposed):
    tile = (2, size.width, size.unit_rows) if transposed else (2, size.unit_rows, size.width)
    return pl.pallas_call(
        functools.partial(pack_kernel, size, transposed),
        out_shape=[
            jax.ShapeDtypeStruct((size.main,) + tile, x.dtype),
            jax.ShapeDtypeStruct((max(size.units * size.supers - size.main, 1),) + tile, x.dtype),
        ],
        in_specs=[smem(), whole_vmem()],
        out_specs=[whole_vmem()] * 2,
        compiler_params=params(),
        cost_estimate=cost(1000, 1000),
        name="pack",
    )(slot, x)


def blank(like):
    return pl.pallas_call(
        lambda *refs: None,
        out_shape=tuple(like),
        out_specs=[any_space()] * len(like),
        compiler_params=params(has_side_effects=True),
        name="blank",
    )()


def swap(x, axis):
    return lax.ppermute(x, axis, [(0, 1), (1, 0)])


def hop(pair, axis, n, t):
    if n == 2:
        return (swap(pair[0], axis),)
    right = lax.ppermute(pair[0], axis, [(i, i + 1) for i in range(t - 1, n - 1)])
    left = lax.ppermute(pair[-1], axis, [(i + 1, i) for i in range(0, n - t)])
    return (right, left)


def line_gather(x, axis, n):
    hops = [(x,)]
    for t in range(1, n):
        hops.append(hop(hops[-1], axis, n, t))
    return hops[1:]


def hop_sources(index, n):
    if n == 2:
        return [(1 - index,)]
    return [
        (jnp.where(index - t >= 0, index - t, -1), jnp.where(index + t < n, index + t, -1)) for t in range(1, n)
    ]


def pick(shards, d):
    return lax.dynamic_index_in_dim(shards, d, 0, keepdims=False)


CODE_ROWS = 16


def decoded(codes, exponents):
    return codes.astype(jnp.int32).astype(F32) * jnp.exp2(exponents[:1].astype(jnp.int32).astype(F32))


def shard_specs(terms, shape, place):
    return [pl.BlockSpec((1,) + shape, lambda j, at: (at[0],) + place(j))] * len(terms)


def term_sum(n_term, refs):
    return functools.reduce(jnp.add, [ref[0] for ref in refs[:n_term]]), refs[n_term:]


def pick_kernel(n_term, rows, index_ref, *refs):
    total, refs = term_sum(n_term, refs)
    for ref in refs[:-1]:
        total = total + decoded(ref[:rows, :], ref[rows:, :])
    out = refs[-1]
    most = jnp.maximum(jnp.max(jnp.abs(total), axis=0, keepdims=True), 1e-30)
    exponent = jnp.ceil(jnp.log2(most) + 0.01) - 15.0
    codes = jnp.floor(total / jnp.exp2(exponent) + 0.5)
    out[:rows, :] = jnp.clip(codes, -32767.0, 32767.0).astype(jnp.int32).astype(jnp.int16)
    out[rows:, :] = jnp.broadcast_to(exponent, (CODE_ROWS, exponent.shape[1])).astype(jnp.int32).astype(jnp.int16)


def pick_coded(terms, d, extra=()):
    rows, w = terms[0].shape[1:]
    step = 256 if w % 256 == 0 else w
    coded = pl.BlockSpec((rows + CODE_ROWS, step), lambda j, at: (0, j))
    return pl.pallas_call(
        functools.partial(pick_kernel, len(terms), rows),
        out_shape=jax.ShapeDtypeStruct((rows + CODE_ROWS, w), jnp.int16),
        grid_spec=pltpu.PrefetchScalarGridSpec(
            num_scalar_prefetch=1,
            grid=(w // step,),
            in_specs=shard_specs(terms, (rows, step), lambda j: (0, j)) + [coded] * len(extra),
            out_specs=coded,
        ),
        compiler_params=params(),
        cost_estimate=cost(1000, 1000),
        name="pick_coded",
    )(jnp.asarray(d, jnp.int32).reshape(1), *terms, *extra)


def finish_kernel(n_term, transposed, index_ref, *refs):
    total, refs = term_sum(n_term, refs)
    coded = refs[:-1]
    for codes, exponents in zip(coded[::2], coded[1::2]):
        total = total + decoded(codes[...], exponents[...])
    refs[-1][0] = total.T if transposed else total


def finish(terms, d, extra, supers, width, transposed):
    rows, w = terms[0].shape[1:]
    share = w if transposed else rows
    tall = rows // CODE_ROWS
    if transposed:
        term = shard_specs(terms, (width, w), lambda s: (s, 0))
        codes = pl.BlockSpec((width, w), lambda s, at: (s, 0))
        exponents = pl.BlockSpec((CODE_ROWS, w), lambda s, at: (tall, 0))
    else:
        term = shard_specs(terms, (rows, width), lambda s: (0, s))
        codes = pl.BlockSpec((rows, width), lambda s, at: (0, s))
        exponents = pl.BlockSpec((CODE_ROWS, width), lambda s, at: (tall, s))
    total = pl.pallas_call(
        functools.partial(finish_kernel, len(terms), transposed),
        out_shape=jax.ShapeDtypeStruct((supers, share, width), F32),
        grid_spec=pltpu.PrefetchScalarGridSpec(
            num_scalar_prefetch=1,
            grid=(supers,),
            in_specs=term + [codes, exponents] * len(extra),
            out_specs=pl.BlockSpec((1, share, width), lambda s, at: (s, 0, 0)),
        ),
        compiler_params=params(),
        cost_estimate=cost(1000, 1000),
        name="finish",
    )(jnp.asarray(d, jnp.int32).reshape(1), *terms, *[x for x in extra for _ in range(2)])
    return jnp.transpose(total, (1, 0, 2))


def scatter_codes(terms, carried, axis, n, t):
    i = lax.axis_index(axis)
    if n == 2:
        return (pick_coded(terms, 1 - i),)
    right = pick_coded(terms, jnp.clip(n - 1 - t + i, 0, n - 1), carried[:1])
    left = pick_coded(terms, jnp.clip(t - (n - 1 - i), 0, n - 1), carried[1:])
    return (right, left)


def scatter_move(codes, axis, n, t):
    if n == 2:
        return (swap(codes[0], axis),)
    right = lax.ppermute(codes[0], axis, [(j, j + 1) for j in range(t + 1)])
    left = lax.ppermute(codes[1], axis, [(n - 1 - j, n - 2 - j) for j in range(t + 1)])
    return (right, left)


def direct_sum(x, axis, n):
    if n & (n - 1):
        return lax.psum(x, axis)
    k = 1
    while k < n:
        x = x + lax.ppermute(x, axis, [(j, j ^ k) for j in range(n)])
        k *= 2
    return x


def halves_back(x, axis, n):
    if n != 2:
        return lax.all_gather(x, axis, axis=0, tiled=True)
    other = lax.ppermute(x, axis, [(0, 1), (1, 0)])
    swap = lax.axis_index(axis) == 1
    return jnp.concatenate([jnp.where(swap, other, x), jnp.where(swap, x, other)])


def with_unit(size, main_ref, spare_ref, buffer, sem, slot, use):
    @pl.when(jnp.logical_and(slot >= 0, slot < size.main))
    def _():
        use(main_ref[slot, 0], main_ref[slot, 1])

    if size.spare:
        with_spare(size, spare_ref, buffer, sem, slot, use)


def with_spare(size, spare_ref, buffer, sem, slot, use):
    @pl.when(slot >= size.main)
    def _():
        copy = pltpu.make_async_copy(spare_ref.at[slot - size.main], buffer, sem)
        copy.start()
        copy.wait()
        use(buffer[0], buffer[1])


def row_kernel(size, first, paired, share, source_ref, slot_ref, weight_ref, *refs):
    refs = list(refs)
    a_ref, main_ref, spare_ref = refs[:3]
    refs = refs[3:]
    n_out = 2 if paired else 1
    before = None if first else refs[:n_out]
    refs = refs[0 if first else n_out :]
    outs, (left, kept, buffer, sem) = refs[:n_out], refs[n_out:]
    units, supers, half, unit_rows = size.units, size.supers, size.width, size.unit_rows
    deep = 2 * unit_rows
    shard = source_ref[0]

    @pl.when(pl.program_id(0) == 0)
    def _():
        for s in range(supers):
            kept[s, units] = 0
            for u in range(units):
                slot = jnp.where(shard >= 0, slot_ref[(jnp.maximum(shard, 0) * units + u) * supers + s], -1)

                def build(real, imag, s=s, u=u):
                    at = kept[s, units]
                    left[s, at, :half, :unit_rows] = real
                    left[s, at, :half, unit_rows:] = -imag
                    left[s, at, half:, :unit_rows] = imag
                    left[s, at, half:, unit_rows:] = real
                    kept[s, at] = u
                    kept[s, units] = at + 1

                with_unit(size, main_ref, spare_ref, buffer, sem, slot, build)

    pole = source_ref[1]

    def store(s, mix):
        rows = pl.ds(pl.multiple_of(s * half, half), half)
        for part in range(2 if paired else 1):
            value = mix[:, part * share : (part + 1) * share] if paired else mix

            def put(out, old):
                if old is None:
                    out[0, rows, :] = -value
                else:
                    out[0, rows, :] = old[0, rows, :] - value

            if not paired:
                put(outs[0], None if first else before[0])
                continue

            @pl.when(pole == part)
            def _():
                put(outs[0], None if first else before[0])

            @pl.when(pole != part)
            def _():
                put(outs[1], None if first else before[1])

    def one(s, _):
        count = kept[s, units]

        @pl.when(count == 0)
        def _():
            store(s, jnp.zeros((half, a_ref.shape[2]), F32))

        for many in range(1, units + 1):

            @pl.when(count == many)
            def _():
                tall = []
                wide = []
                for i in range(many):
                    rows = pl.ds(pl.multiple_of(kept[s, i] * unit_rows, unit_rows), unit_rows)
                    tall += [a_ref[0, rows, :], a_ref[1, rows, :]]
                    wide.append(left[s, i])
                wide = wide[0] if many == 1 else jnp.concatenate(wide, axis=1)
                sums = jnp.dot(wide, jnp.concatenate(tall, axis=0), preferred_element_type=F32)
                store(s, weight_ref[1] * sums[:half] + weight_ref[0] * sums[half:])

        return 0

    lax.fori_loop(0, supers, one, 0)


def row_product(inverse, before, source, pole, slot, weights, pieces, size, tile, share):
    first = before is None
    part_rows, part_cols = inverse.shape[1:]
    rows = size.units * size.unit_rows
    deep = size.supers * size.width
    count = part_cols // tile
    paired = tile == 2 * share
    thin = share if paired else tile
    n_out = 2 if paired else 1
    tiles = [pl.BlockSpec((1, deep, thin), lambda j, *_: (j, 0, 0))] * n_out
    outs = [jax.ShapeDtypeStruct((count, deep, thin), F32)] * n_out
    return pl.pallas_call(
        functools.partial(row_kernel, size, first, paired, share),
        out_shape=outs,
        grid_spec=pltpu.PrefetchScalarGridSpec(
            num_scalar_prefetch=2,
            grid=(count,),
            in_specs=[smem(), pl.BlockSpec((2, rows, tile), lambda j, src, _: (0, jnp.maximum(src[0], 0), j))]
            + [whole_vmem(), any_space()]
            + ([] if first else tiles),
            out_specs=tiles,
            scratch_shapes=[
                pltpu.VMEM((size.supers, size.units, 2 * size.width, 2 * size.unit_rows), BF16),
                pltpu.SMEM((size.supers, size.units + 1), jnp.int32),
                pltpu.VMEM((2, size.width, size.unit_rows), BF16),
                pltpu.SemaphoreType.DMA,
            ],
        ),
        compiler_params=params(),
        cost_estimate=cost(1000, 1000),
        name="row_product",
    )(jnp.stack([source, pole]), slot, weights, inverse, *pieces, *([] if first else before))


def column_kernel(size, n_source, n_upper, part_rows, n_share, first, last, source_ref, slot_ref, weight_ref, *refs):
    units, supers, width, unit_rows = size.units, size.supers, size.width, size.unit_rows
    refs = list(refs)
    acc_in = None if first else refs.pop(0)
    a_ref = refs.pop(0)
    pieces = [(refs.pop(0), refs.pop(0)) for _ in range(n_source)]
    uppers = [(refs.pop(0), refs.pop(0)) for _ in range(n_upper)]
    if last:
        keep_ref, send_ref, t_ref = refs[:3]
        acc, upper_mains, upper_buffer, upper_sems = refs[3:7]
        refs = refs[7:]
    else:
        acc = refs.pop(0)
    right, mains, buffer, sem, main_sems, acc_sems = refs
    step = pl.program_id(0)
    loads = [pltpu.make_async_copy(pieces[q][0], mains.at[q], main_sems.at[q]) for q in range(n_source)]
    acc_loads = []
    if not first:
        acc_loads = [pltpu.make_async_copy(acc_in.at[s], acc.at[s], acc_sems.at[s]) for s in range(supers)]
    upper_loads = [pltpu.make_async_copy(uppers[q][0], upper_mains.at[q], upper_sems.at[q]) for q in range(n_upper)]

    @pl.when(step == 0)
    def _():
        for load in loads[:1] + acc_loads + loads[1:] + upper_loads:
            load.start()
        if first:
            acc[...] = jnp.zeros_like(acc)

    for q in range(n_source):

        @pl.when(step == q * units)
        def _():
            loads[q].wait()

    source = step // units
    shard = source_ref[source]
    place = jnp.maximum(shard, 0) * units + step % units

    for s in range(supers):
        slot = jnp.where(shard >= 0, slot_ref[place * supers + s], -1)

        def build(real, imag):
            right[:unit_rows, :width] = real
            right[:unit_rows, width:] = imag
            right[unit_rows:, :width] = -imag
            right[unit_rows:, width:] = real

        @pl.when(jnp.logical_and(slot >= 0, slot < size.main))
        def _():
            build(mains[source, slot, 0], mains[source, slot, 1])

        if size.spare:
            for q in range(n_source):
                with_spare(size, pieces[q][1], buffer, sem, jnp.where(source == q, slot, -1), build)

        if not first:

            @pl.when(step == 0)
            def _():
                acc_loads[s].wait()

        @pl.when(slot >= 0)
        def _():
            both = jnp.concatenate([a_ref[0], a_ref[1]], axis=1)
            acc[s] += jnp.dot(both, right[...], preferred_element_type=F32)

    if not last:
        return

    @pl.when(step == n_source * units - 1)
    def _():
        weight_real = weight_ref[0]
        weight_imag = weight_ref[1]
        pole = source_ref[n_source + n_upper]
        share = part_rows // n_share
        for load in upper_loads:
            load.wait()
        for k in range(n_share):
            rows = slice(k * share, (k + 1) * share)
            for part, out in ((0, keep_ref), (1, send_ref)):

                @pl.when((pole == k % 2) == (part == 0))
                def _():
                    for s in range(supers):
                        out[k // 2, :, s * width : (s + 1) * width] = -(
                            weight_imag * acc[s, rows, :width] + weight_real * acc[s, rows, width:]
                        )

        t_ref[...] = jnp.zeros_like(t_ref)

        def unit(k, _):
            rows = pl.ds(pl.multiple_of(k * unit_rows, unit_rows), unit_rows)
            upper = jnp.int32(0)
            for q in range(n_upper):
                upper = jnp.where(source_ref[n_source + q] == k // units, q, upper)
            for s in range(supers):
                slot = slot_ref[n_slots + k * supers + s]

                def use(real, imag):
                    first_acc = acc[s, rows, :width]
                    second_acc = acc[s, rows, width:]
                    mix = weight_imag * first_acc + weight_real * second_acc
                    other = weight_real * first_acc - weight_imag * second_acc
                    stacked = jnp.concatenate([mix, other], axis=0)
                    high = stacked.astype(BF16)
                    low = (stacked - high.astype(F32)).astype(BF16)
                    both = jnp.concatenate([real, imag], axis=1)
                    sums = jnp.dot(both, jnp.concatenate([high, low], axis=1), preferred_element_type=F32)
                    t_ref[s] += sums[:, :width] + sums[:, width:]

                @pl.when(jnp.logical_and(slot >= 0, slot < size.main))
                def _():
                    use(upper_mains[upper, slot, 0], upper_mains[upper, slot, 1])

                if size.spare:
                    for q in range(n_upper):
                        with_spare(size, uppers[q][1], upper_buffer, sem, jnp.where(upper == q, slot, -1), use)

            return 0

        n_slots = slot_ref.shape[0] - part_rows // unit_rows * supers
        lax.fori_loop(0, part_rows // unit_rows, unit, 0)


def column_phase(inverse, acc, sources, positions, slot, weights, pieces, uppers, size, n_col):
    first, last = acc is None, bool(uppers)
    n_source, n_upper = len(pieces), len(uppers)
    part_rows, part_cols = inverse.shape[1:]
    units, unit_rows, supers, width = size.units, size.unit_rows, size.supers, size.width
    flat = [p for group in pieces + uppers for p in group]

    steps = []
    for q in range(n_source):
        idle = jnp.int32(0)
        for other in [*range(n_source - 1, q, -1), *range(q)]:
            edge = sources[other] * units + (units - 1 if other < q else 0)
            idle = jnp.where(sources[other] >= 0, edge, idle)
        steps.append(jnp.where(sources[q] >= 0, sources[q] * units + lax.iota(jnp.int32, units), idle))
    prefetch = jnp.concatenate([jnp.stack(sources + positions)] + steps)

    def a_map(g, src, _):
        return (0, 0, src[len(sources) + len(positions) + g])

    acc_shape = (supers, part_rows, 2 * width)
    in_specs = [smem()] + ([] if first else [any_space()])
    in_specs += [pl.BlockSpec((2, part_rows, unit_rows), a_map)] + [any_space()] * len(flat)
    scratch = [
        pltpu.VMEM((2 * unit_rows, 2 * width), BF16),
        pltpu.VMEM((n_source, size.main, 2, unit_rows, width), BF16),
        pltpu.VMEM((2, unit_rows, width), BF16),
        pltpu.SemaphoreType.DMA,
        pltpu.SemaphoreType.DMA((n_source,)),
        pltpu.SemaphoreType.DMA((supers,)),
    ]
    if last:
        out_shape = [jax.ShapeDtypeStruct((n_col, part_rows // (2 * n_col), supers * width), F32)] * 2
        out_shape.append(jax.ShapeDtypeStruct((supers, width, width), F32))
        scratch = [
            pltpu.VMEM(acc_shape, F32),
            pltpu.VMEM((n_upper, size.main, 2, width, unit_rows), BF16),
            pltpu.VMEM((2, width, unit_rows), BF16),
            pltpu.SemaphoreType.DMA((n_upper,)),
        ] + scratch
    else:
        out_shape = [jax.ShapeDtypeStruct(acc_shape, F32)]
    return pl.pallas_call(
        functools.partial(column_kernel, size, n_source, n_upper, part_rows, 2 * n_col, first, last),
        out_shape=out_shape,
        grid_spec=pltpu.PrefetchScalarGridSpec(
            num_scalar_prefetch=2,
            grid=(n_source * units,),
            in_specs=in_specs,
            out_specs=[whole_vmem()] * len(out_shape),
            scratch_shapes=scratch,
        ),
        compiler_params=params(),
        cost_estimate=cost(1000, 1000),
        name="column_phase",
    )(prefetch, slot, weights, *([] if first else [acc]), inverse, *flat)


def body(inverse, lower, upper, diag_inverse, weights, pattern):
    n_group = lax.axis_size("groups")
    n_row = lax.axis_size("row")
    n_col = lax.axis_size("col")
    n_pole = lax.axis_size("pole")
    assert n_pole == 2
    row_index = lax.axis_index("row")
    col_index = lax.axis_index("col")
    pole_index = lax.axis_index("pole")
    local_rows, _, supers, width = lower.shape[1:]
    inverse = inverse[0]
    part_rows, part_cols = inverse.shape[1:]
    unit_rows = min(width, local_rows)
    units = local_rows // unit_rows
    size = Sizes(units, supers, unit_rows, width)
    weight = weights[0]
    lower_from = [(row_index,)] + hop_sources(row_index, n_row)
    upper_from = [p for pair in hop_sources(col_index, n_col) for p in pair]

    slot, most = unit_tables(pattern, n_row * n_col, units, unit_rows, width)
    most = most.astype(F32)
    for k in range(1, n_group):
        most = jnp.maximum(most, lax.ppermute(most, "groups", [(j, (j + k) % n_group) for j in range(n_group)]))
    row_slot = lax.dynamic_slice_in_dim(slot, row_index * n_col, n_col, 0).reshape(-1)
    col_slot = lax.dynamic_slice_in_dim(slot, col_index * n_row, n_row, 0).reshape(-1)
    lower_parts = jnp.transpose(lower[0], (1, 2, 0, 3))
    own_lower, spare_lower = pack(lower_parts, pick(slot, col_index * n_row + row_index), size, False)
    own_lower, spare_lower, upper, most = fence((own_lower, spare_lower, upper, most))

    def first_part(size):
        def run(upper, own_lower, spare_lower):
            upper_parts = jnp.transpose(upper[0], (1, 2, 0, 3))
            own_upper = pack(upper_parts, pick(slot, row_index * n_col + col_index), size, True)
            got = [p for pair in line_gather(own_upper[0], "col", n_col) for p in pair]
            sums = row_product(inverse, None, col_index, pole_index, row_slot, weight, own_upper, size, tile, share)
            sums, own_lower = fence((sums, own_lower))
            pieces = [(own_lower, spare_lower)]
            acc, = column_phase(inverse, None, [row_index], [], col_slot, weight, pieces, [], size, n_col)
            return own_upper, got, sums, acc

        return run

    tile = min(1024, part_cols)
    share = part_cols // (n_row * n_pole)
    crowded = most > size.main
    passing = hop((own_lower,), "row", n_row, 1)
    own_upper, upper_got, sums, acc = lax.cond(
        crowded, first_part(size), first_part(size.usual()), upper, own_lower, spare_lower
    )
    passing, own_upper, upper_got, sums, acc = fence((passing, own_upper, upper_got, sums, acc))

    def send(pieces):
        return jax.tree.leaves([line_gather(pieces[0], "row", n_row), line_gather(pieces[1], "col", n_col)])

    def skip(pieces):
        return list(blank(jax.eval_shape(send, pieces)))

    spread = lax.cond(crowded, send, skip, (spare_lower, own_upper[1]))
    row_spares, col_spares = spread[: len(spread) - len(upper_got)], spread[len(spread) - len(upper_got) :]
    uppers = [own_upper] + list(zip(upper_got, col_spares))

    def second_part(size):
        def run(sums, got, col_spares):
            for source, *pieces in zip(upper_from, got, col_spares):
                sums = row_product(inverse, sums, source, pole_index, row_slot, weight, pieces, size, tile, share)
            if len(sums) == 2:
                terms = (sums[0], swap(sums[1], "pole"))
            else:
                both = jnp.transpose(sums[0], (1, 0, 2)).reshape(supers * width, n_row, n_pole, share)
                both = jnp.transpose(both, (2, 1, 0, 3))
                terms = (pick(both, pole_index), swap(pick(both, 1 - pole_index), "pole"))
            return terms, scatter_codes(terms, (), "row", n_row, 0)

        return run

    held = [(1, passing)]
    if n_row > 2:
        passing = hop(passing, "row", n_row, 2)
    terms, codes = lax.cond(
        crowded, second_part(size), second_part(size.usual()), sums, upper_got, col_spares
    )
    passing, terms, codes = fence((passing, terms, codes))

    def spare_pair(t):
        return row_spares[(t - 1) * len(held[-1][1]) : t * len(held[-1][1])]

    def phase(acc, held, last):
        sources = [p for t, _ in held for p in lower_from[t]]
        pieces = [p for t, pair in held for p in zip(pair, spare_pair(t) if t else [spare_lower])]
        if not last:
            return column_phase(inverse, acc, sources, [], col_slot, weight, pieces, [], size, n_col)
        positions = [col_index] + upper_from + [pole_index]
        slots = jnp.concatenate([col_slot, row_slot])
        return column_phase(inverse, acc, sources, positions, slots, weight, pieces, uppers, size, n_col)

    stage = 0
    for t in range(3, n_row):
        held.append((t - 1, passing))
        passing = hop(passing, "row", n_row, t)
        carried = scatter_move(codes, "row", n_row, stage)
        stage += 1
        if t == n_row - 1:
            acc, = phase(acc, held, False)
            held = []
        codes = scatter_codes(terms, carried, "row", n_row, stage)
        passing, acc, terms, codes = fence((passing, acc, terms, codes))
    if n_row > 2:
        held.append((n_row - 1, passing))
    if stage < n_row - 2:
        carried = scatter_move(codes, "row", n_row, stage)
        stage += 1
        codes = scatter_codes(terms, carried, "row", n_row, stage)
    keep, give, t_part = phase(acc, held, True)
    keep, give, t_part, terms, codes = fence((keep, give, t_part, terms, codes))

    col_terms = (keep, swap(give, "pole"))
    while stage < n_row - 1:
        carried = scatter_move(codes, "row", n_row, stage)
        stage += 1
        if stage < n_row - 1:
            codes = scatter_codes(terms, carried, "row", n_row, stage)
    col_codes = scatter_codes(col_terms, (), "col", n_col, 0)

    given = diag_inverse[0].astype(F32)
    own_term = weight[0] * given[:, 1] + weight[1] * given[:, 0]
    owner = jnp.logical_and(row_index == 0, col_index == 0)
    t_part = (t_part + jnp.where(owner, own_term, 0.0)).reshape(n_pole, -1, width)
    t_sum = pick(t_part, pole_index) + swap(pick(t_part, 1 - pole_index), "pole")
    if n_col == 2:
        t_sum = t_sum.reshape(n_col, -1, width)
        t_sum = pick(t_sum, col_index) + swap(pick(t_sum, 1 - col_index), "col")
    else:
        t_sum = direct_sum(t_sum, "col", n_col)
    t_sum, col_codes = fence((t_sum, col_codes))
    for t in range(n_col - 1):
        col_carried = scatter_move(col_codes, "col", n_col, t)
        if t < n_col - 2:
            col_codes = scatter_codes(col_terms, col_carried, "col", n_col, t + 1)
    t_sum = direct_sum(t_sum, "row", n_row)
    t_sum, col_carried, carried = fence((t_sum, col_carried, carried))
    if n_col == 2:
        t_sum = halves_back(t_sum, "col", n_col)
    diagonal_density = halves_back(t_sum, "pole", n_pole).reshape(supers, width, width)
    column_density = finish(col_terms, col_index, col_carried, supers, width, False)
    row_density = finish(terms, row_index, carried, supers, width, True)
    return (column_density, row_density, diagonal_density)


def solution(mesh):
    return jax.shard_map(
        body,
        mesh=mesh,
        in_specs=(
            P(("groups", "pole"), None, "row", "col"),
            P(("groups", "pole"), ("col", "row"), None, None, None),
            P(("groups", "pole"), ("row", "col"), None, None, None),
            P(("groups", "pole"), None, None, None, None),
            P(("groups", "pole"), None),
            P("groups", None),
        ),
        out_specs=(
            P(("groups", "row", "col", "pole"), None, None),
            P(("groups", "col", "row", "pole"), None, None),
            P("groups", None, None),
        ),
        check_vma=False,
    )
```

```python
import functools

import jax
import jax.numpy as jnp
from jax import lax
from jax.experimental import pallas as pl
from jax.experimental.pallas import tpu as pltpu
from jax.sharding import PartitionSpec as P

VMEM_LIMIT = 46 * 1024 * 1024
F32 = jnp.float32
BF16 = jnp.bfloat16


def params(limit=VMEM_LIMIT, **kw):
    return pltpu.CompilerParams(vmem_limit_bytes=limit, **kw)


def cost(flops, nbytes):
    return pl.CostEstimate(flops=int(flops), bytes_accessed=int(nbytes), transcendentals=0)


def fence(tree):
    return lax.optimization_barrier(tree)


def whole_vmem():
    return pl.BlockSpec(memory_space=pltpu.VMEM)


def smem():
    return pl.BlockSpec(memory_space=pltpu.SMEM)


def unit_tables(pattern, shards, units, unit_rows, width):
    supers = pattern.shape[0]
    block = (lax.iota(jnp.int32, shards * units) * unit_rows) // width
    hits = jnp.any(pattern[:, :, None] == block[None, None, :], axis=1)
    flags = jnp.transpose(hits).reshape(shards, units * supers).astype(jnp.int32)
    places = lax.iota(jnp.int32, units * supers)
    before = (places[:, None] < places[None, :]).astype(jnp.int32)
    rank = jnp.sum(flags[:, :, None] * before[None], axis=1)
    slot = jnp.where(flags > 0, rank, -1)
    most = jnp.max(jnp.sum(flags, axis=1))
    return slot, most


class Sizes:
    def __init__(self, units, supers, unit_rows, width):
        self.units, self.supers, self.unit_rows, self.width = units, supers, unit_rows, width
        self.main = units * max(supers - 1, 1)
        self.spare = units * supers - self.main

    def usual(self):
        size = Sizes(self.units, self.supers, self.unit_rows, self.width)
        size.spare = 0
        return size


def any_space():
    return pl.BlockSpec(memory_space=pl.ANY)


def pack_kernel(size, transposed, slot_ref, x_ref, main_ref, spare_ref):
    rows = size.unit_rows
    for u in range(size.units):
        for s in range(size.supers):
            slot = slot_ref[u * size.supers + s]

            def store(ref, at):
                for h in range(2):
                    tile = x_ref[h, s, u * rows : (u + 1) * rows, :]
                    ref[at, h] = tile.T if transposed else tile

            @pl.when(jnp.logical_and(slot >= 0, slot < size.main))
            def _():
                store(main_ref, slot)

            if size.spare:

                @pl.when(slot >= size.main)
                def _():
                    store(spare_ref, slot - size.main)


def pack(x, slot, size, transposed):
    tile = (2, size.width, size.unit_rows) if transposed else (2, size.unit_rows, size.width)
    return pl.pallas_call(
        functools.partial(pack_kernel, size, transposed),
        out_shape=[
            jax.ShapeDtypeStruct((size.main,) + tile, x.dtype),
            jax.ShapeDtypeStruct((max(size.units * size.supers - size.main, 1),) + tile, x.dtype),
        ],
        in_specs=[smem(), whole_vmem()],
        out_specs=[whole_vmem()] * 2,
        compiler_params=params(),
        cost_estimate=cost(1000, 1000),
        name="pack",
    )(slot, x)


def blank(like):
    return pl.pallas_call(
        lambda *refs: None,
        out_shape=tuple(like),
        out_specs=[any_space()] * len(like),
        compiler_params=params(has_side_effects=True),
        name="blank",
    )()


def swap(x, axis):
    return lax.ppermute(x, axis, [(0, 1), (1, 0)])


def hop(pair, axis, n, t):
    if n == 2:
        return (swap(pair[0], axis),)
    right = lax.ppermute(pair[0], axis, [(i, i + 1) for i in range(t - 1, n - 1)])
    left = lax.ppermute(pair[-1], axis, [(i + 1, i) for i in range(0, n - t)])
    return (right, left)


def line_gather(x, axis, n):
    hops = [(x,)]
    for t in range(1, n):
        hops.append(hop(hops[-1], axis, n, t))
    return hops[1:]


def hop_sources(index, n):
    if n == 2:
        return [(1 - index,)]
    return [
        (jnp.where(index - t >= 0, index - t, -1), jnp.where(index + t < n, index + t, -1)) for t in range(1, n)
    ]


def pick(shards, d):
    return lax.dynamic_index_in_dim(shards, d, 0, keepdims=False)


CODE_ROWS = 16


def decoded(codes, exponents):
    return codes.astype(jnp.int32).astype(F32) * jnp.exp2(exponents[:1].astype(jnp.int32).astype(F32))


def shard_specs(terms, shape, place):
    return [pl.BlockSpec((1,) + shape, lambda j, at: (at[0],) + place(j))] * len(terms)


def term_sum(n_term, refs):
    return functools.reduce(jnp.add, [ref[0] for ref in refs[:n_term]]), refs[n_term:]


def pick_kernel(n_term, rows, index_ref, *refs):
    total, refs = term_sum(n_term, refs)
    for ref in refs[:-1]:
        total = total + decoded(ref[:rows, :], ref[rows:, :])
    out = refs[-1]
    most = jnp.maximum(jnp.max(jnp.abs(total), axis=0, keepdims=True), 1e-30)
    exponent = jnp.ceil(jnp.log2(most) + 0.01) - 15.0
    codes = jnp.floor(total / jnp.exp2(exponent) + 0.5)
    out[:rows, :] = jnp.clip(codes, -32767.0, 32767.0).astype(jnp.int32).astype(jnp.int16)
    out[rows:, :] = jnp.broadcast_to(exponent, (CODE_ROWS, exponent.shape[1])).astype(jnp.int32).astype(jnp.int16)


def pick_coded(terms, d, extra=()):
    rows, w = terms[0].shape[1:]
    step = 256 if w % 256 == 0 else w
    coded = pl.BlockSpec((rows + CODE_ROWS, step), lambda j, at: (0, j))
    return pl.pallas_call(
        functools.partial(pick_kernel, len(terms), rows),
        out_shape=jax.ShapeDtypeStruct((rows + CODE_ROWS, w), jnp.int16),
        grid_spec=pltpu.PrefetchScalarGridSpec(
            num_scalar_prefetch=1,
            grid=(w // step,),
            in_specs=shard_specs(terms, (rows, step), lambda j: (0, j)) + [coded] * len(extra),
            out_specs=coded,
        ),
        compiler_params=params(),
        cost_estimate=cost(1000, 1000),
        name="pick_coded",
    )(jnp.asarray(d, jnp.int32).reshape(1), *terms, *extra)


def finish_kernel(n_term, transposed, index_ref, *refs):
    total, refs = term_sum(n_term, refs)
    coded = refs[:-1]
    for codes, exponents in zip(coded[::2], coded[1::2]):
        total = total + decoded(codes[...], exponents[...])
    refs[-1][0] = total.T if transposed else total


def finish(terms, d, extra, supers, width, transposed):
    rows, w = terms[0].shape[1:]
    share = w if transposed else rows
    tall = rows // CODE_ROWS
    if transposed:
        term = shard_specs(terms, (width, w), lambda s: (s, 0))
        codes = pl.BlockSpec((width, w), lambda s, at: (s, 0))
        exponents = pl.BlockSpec((CODE_ROWS, w), lambda s, at: (tall, 0))
    else:
        term = shard_specs(terms, (rows, width), lambda s: (0, s))
        codes = pl.BlockSpec((rows, width), lambda s, at: (0, s))
        exponents = pl.BlockSpec((CODE_ROWS, width), lambda s, at: (tall, s))
    total = pl.pallas_call(
        functools.partial(finish_kernel, len(terms), transposed),
        out_shape=jax.ShapeDtypeStruct((supers, share, width), F32),
        grid_spec=pltpu.PrefetchScalarGridSpec(
            num_scalar_prefetch=1,
            grid=(supers,),
            in_specs=term + [codes, exponents] * len(extra),
            out_specs=pl.BlockSpec((1, share, width), lambda s, at: (s, 0, 0)),
        ),
        compiler_params=params(),
        cost_estimate=cost(1000, 1000),
        name="finish",
    )(jnp.asarray(d, jnp.int32).reshape(1), *terms, *[x for x in extra for _ in range(2)])
    return jnp.transpose(total, (1, 0, 2))


def scatter_codes(terms, carried, axis, n, t):
    i = lax.axis_index(axis)
    if n == 2:
        return (pick_coded(terms, 1 - i),)
    right = pick_coded(terms, jnp.clip(n - 1 - t + i, 0, n - 1), carried[:1])
    left = pick_coded(terms, jnp.clip(t - (n - 1 - i), 0, n - 1), carried[1:])
    return (right, left)


def scatter_move(codes, axis, n, t):
    if n == 2:
        return (swap(codes[0], axis),)
    right = lax.ppermute(codes[0], axis, [(j, j + 1) for j in range(t + 1)])
    left = lax.ppermute(codes[1], axis, [(n - 1 - j, n - 2 - j) for j in range(t + 1)])
    return (right, left)


def direct_sum(x, axis, n):
    if n & (n - 1):
        return lax.psum(x, axis)
    k = 1
    while k < n:
        x = x + lax.ppermute(x, axis, [(j, j ^ k) for j in range(n)])
        k *= 2
    return x


def halves_back(x, axis, n):
    if n != 2:
        return lax.all_gather(x, axis, axis=0, tiled=True)
    other = lax.ppermute(x, axis, [(0, 1), (1, 0)])
    swap = lax.axis_index(axis) == 1
    return jnp.concatenate([jnp.where(swap, other, x), jnp.where(swap, x, other)])


def with_unit(size, main_ref, spare_ref, buffer, sem, slot, use):
    @pl.when(jnp.logical_and(slot >= 0, slot < size.main))
    def _():
        use(main_ref[slot, 0], main_ref[slot, 1])

    if size.spare:
        with_spare(size, spare_ref, buffer, sem, slot, use)


def with_spare(size, spare_ref, buffer, sem, slot, use):
    @pl.when(slot >= size.main)
    def _():
        copy = pltpu.make_async_copy(spare_ref.at[slot - size.main], buffer, sem)
        copy.start()
        copy.wait()
        use(buffer[0], buffer[1])


def row_kernel(size, first, paired, share, source_ref, slot_ref, weight_ref, *refs):
    refs = list(refs)
    a_ref, main_ref, spare_ref = refs[:3]
    refs = refs[3:]
    n_out = 2 if paired else 1
    before = None if first else refs[:n_out]
    refs = refs[0 if first else n_out :]
    outs, (left, kept, buffer, sem) = refs[:n_out], refs[n_out:]
    units, supers, half, unit_rows = size.units, size.supers, size.width, size.unit_rows
    deep = 2 * unit_rows
    shard = source_ref[0]

    @pl.when(pl.program_id(0) == 0)
    def _():
        for s in range(supers):
            kept[s, units] = 0
            for u in range(units):
                slot = jnp.where(shard >= 0, slot_ref[(jnp.maximum(shard, 0) * units + u) * supers + s], -1)

                def build(real, imag, s=s, u=u):
                    at = kept[s, units]
                    left[s, at, :half, :unit_rows] = real
                    left[s, at, :half, unit_rows:] = -imag
                    left[s, at, half:, :unit_rows] = imag
                    left[s, at, half:, unit_rows:] = real
                    kept[s, at] = u
                    kept[s, units] = at + 1

                with_unit(size, main_ref, spare_ref, buffer, sem, slot, build)

    pole = source_ref[1]

    def store(s, mix):
        rows = pl.ds(pl.multiple_of(s * half, half), half)
        for part in range(2 if paired else 1):
            value = mix[:, part * share : (part + 1) * share] if paired else mix

            def put(out, old):
                if old is None:
                    out[0, rows, :] = -value
                else:
                    out[0, rows, :] = old[0, rows, :] - value

            if not paired:
                put(outs[0], None if first else before[0])
                continue

            @pl.when(pole == part)
            def _():
                put(outs[0], None if first else before[0])

            @pl.when(pole != part)
            def _():
                put(outs[1], None if first else before[1])

    def one(s, _):
        count = kept[s, units]

        @pl.when(count == 0)
        def _():
            store(s, jnp.zeros((half, a_ref.shape[2]), F32))

        for many in range(1, units + 1):

            @pl.when(count == many)
            def _():
                tall = []
                wide = []
                for i in range(many):
                    rows = pl.ds(pl.multiple_of(kept[s, i] * unit_rows, unit_rows), unit_rows)
                    tall += [a_ref[0, rows, :], a_ref[1, rows, :]]
                    wide.append(left[s, i])
                wide = wide[0] if many == 1 else jnp.concatenate(wide, axis=1)
                sums = jnp.dot(wide, jnp.concatenate(tall, axis=0), preferred_element_type=F32)
                store(s, weight_ref[1] * sums[:half] + weight_ref[0] * sums[half:])

        return 0

    lax.fori_loop(0, supers, one, 0)


def row_product(inverse, before, source, pole, slot, weights, pieces, size, tile, share):
    first = before is None
    part_rows, part_cols = inverse.shape[1:]
    rows = size.units * size.unit_rows
    deep = size.supers * size.width
    count = part_cols // tile
    paired = tile == 2 * share
    thin = share if paired else tile
    n_out = 2 if paired else 1
    tiles = [pl.BlockSpec((1, deep, thin), lambda j, *_: (j, 0, 0))] * n_out
    outs = [jax.ShapeDtypeStruct((count, deep, thin), F32)] * n_out
    return pl.pallas_call(
        functools.partial(row_kernel, size, first, paired, share),
        out_shape=outs,
        grid_spec=pltpu.PrefetchScalarGridSpec(
            num_scalar_prefetch=2,
            grid=(count,),
            in_specs=[smem(), pl.BlockSpec((2, rows, tile), lambda j, src, _: (0, jnp.maximum(src[0], 0), j))]
            + [whole_vmem(), any_space()]
            + ([] if first else tiles),
            out_specs=tiles,
            scratch_shapes=[
                pltpu.VMEM((size.supers, size.units, 2 * size.width, 2 * size.unit_rows), BF16),
                pltpu.SMEM((size.supers, size.units + 1), jnp.int32),
                pltpu.VMEM((2, size.width, size.unit_rows), BF16),
                pltpu.SemaphoreType.DMA,
            ],
        ),
        compiler_params=params(),
        cost_estimate=cost(1000, 1000),
        name="row_product",
    )(jnp.stack([source, pole]), slot, weights, inverse, *pieces, *([] if first else before))


def column_kernel(size, n_source, n_upper, n_after, part_rows, n_share, first, last, source_ref, slot_ref, weight_ref, *refs):
    units, supers, width, unit_rows = size.units, size.supers, size.width, size.unit_rows
    refs = list(refs)
    if not first:
        refs.pop(0)
    a_ref = refs.pop(0)
    pieces = [(refs.pop(0), refs.pop(0)) for _ in range(n_source)]
    uppers = [(refs.pop(0), refs.pop(0)) for _ in range(n_upper)]
    refs = refs[n_after:]
    if last:
        acc, keep_ref, send_ref, t_ref = refs[:4]
        upper_mains, upper_buffer, upper_sems = refs[4:7]
        refs = refs[7:]
    else:
        acc, token_ref = refs.pop(0), refs.pop(0)
    right, mains, buffer, sem, main_sems = refs
    step = pl.program_id(0)
    loads = [pltpu.make_async_copy(pieces[q][0], mains.at[q], main_sems.at[q]) for q in range(n_source)]
    upper_loads = [pltpu.make_async_copy(uppers[q][0], upper_mains.at[q], upper_sems.at[q]) for q in range(n_upper)]

    @pl.when(step == 0)
    def _():
        for load in loads + upper_loads:
            load.start()
        if not last:
            token_ref[...] = jnp.zeros_like(token_ref)
        if first:
            acc[...] = jnp.zeros_like(acc)

    for q in range(n_source):

        @pl.when(step == q * units)
        def _():
            loads[q].wait()

    source = step // units
    shard = source_ref[source]
    place = jnp.maximum(shard, 0) * units + step % units

    for s in range(supers):
        slot = jnp.where(shard >= 0, slot_ref[place * supers + s], -1)

        def build(real, imag):
            right[:unit_rows, :width] = real
            right[:unit_rows, width:] = imag
            right[unit_rows:, :width] = -imag
            right[unit_rows:, width:] = real

        @pl.when(jnp.logical_and(slot >= 0, slot < size.main))
        def _():
            build(mains[source, slot, 0], mains[source, slot, 1])

        if size.spare:
            for q in range(n_source):
                with_spare(size, pieces[q][1], buffer, sem, jnp.where(source == q, slot, -1), build)

        @pl.when(slot >= 0)
        def _():
            both = jnp.concatenate([a_ref[0], a_ref[1]], axis=1)
            acc[s] += jnp.dot(both, right[...], preferred_element_type=F32)

    if not last:
        return

    @pl.when(step == n_source * units - 1)
    def _():
        weight_real = weight_ref[0]
        weight_imag = weight_ref[1]
        pole = source_ref[n_source + n_upper]
        share = part_rows // n_share
        for load in upper_loads:
            load.wait()
        for k in range(n_share):
            rows = slice(k * share, (k + 1) * share)
            for part, out in ((0, keep_ref), (1, send_ref)):

                @pl.when((pole == k % 2) == (part == 0))
                def _():
                    for s in range(supers):
                        out[k // 2, :, s * width : (s + 1) * width] = -(
                            weight_imag * acc[s, rows, :width] + weight_real * acc[s, rows, width:]
                        )

        t_ref[...] = jnp.zeros_like(t_ref)

        def unit(k, _):
            rows = pl.ds(pl.multiple_of(k * unit_rows, unit_rows), unit_rows)
            upper = jnp.int32(0)
            for q in range(n_upper):
                upper = jnp.where(source_ref[n_source + q] == k // units, q, upper)
            for s in range(supers):
                slot = slot_ref[n_slots + k * supers + s]

                def use(real, imag):
                    first_acc = acc[s, rows, :width]
                    second_acc = acc[s, rows, width:]
                    mix = weight_imag * first_acc + weight_real * second_acc
                    other = weight_real * first_acc - weight_imag * second_acc
                    stacked = jnp.concatenate([mix, other], axis=0)
                    high = stacked.astype(BF16)
                    low = (stacked - high.astype(F32)).astype(BF16)
                    both = jnp.concatenate([real, imag], axis=1)
                    sums = jnp.dot(both, jnp.concatenate([high, low], axis=1), preferred_element_type=F32)
                    t_ref[s] += sums[:, :width] + sums[:, width:]

                @pl.when(jnp.logical_and(slot >= 0, slot < size.main))
                def _():
                    use(upper_mains[upper, slot, 0], upper_mains[upper, slot, 1])

                if size.spare:
                    for q in range(n_upper):
                        with_spare(size, uppers[q][1], upper_buffer, sem, jnp.where(upper == q, slot, -1), use)

            return 0

        n_slots = slot_ref.shape[0] - part_rows // unit_rows * supers
        lax.fori_loop(0, part_rows // unit_rows, unit, 0)


def column_phase(inverse, acc, sources, positions, slot, weights, pieces, uppers, size, n_col, after=()):
    first, last = acc is None, bool(uppers)
    n_source, n_upper = len(pieces), len(uppers)
    part_rows, part_cols = inverse.shape[1:]
    units, unit_rows, supers, width = size.units, size.unit_rows, size.supers, size.width
    flat = [p for group in pieces + uppers for p in group]

    steps = []
    for q in range(n_source):
        idle = jnp.int32(0)
        for other in [*range(n_source - 1, q, -1), *range(q)]:
            edge = sources[other] * units + (units - 1 if other < q else 0)
            idle = jnp.where(sources[other] >= 0, edge, idle)
        steps.append(jnp.where(sources[q] >= 0, sources[q] * units + lax.iota(jnp.int32, units), idle))
    prefetch = jnp.concatenate([jnp.stack(sources + positions)] + steps)

    def a_map(g, src, _):
        return (0, 0, src[len(sources) + len(positions) + g])

    acc_shape = (supers, part_rows, 2 * width)
    in_specs = [smem()] + ([] if first else [whole_vmem()])
    if not first:
        acc = pltpu.with_memory_space_constraint(acc, pltpu.VMEM)
    in_specs += [pl.BlockSpec((2, part_rows, unit_rows), a_map)] + [any_space()] * (len(flat) + len(after))
    scratch = [
        pltpu.VMEM((2 * unit_rows, 2 * width), BF16),
        pltpu.VMEM((n_source, size.main, 2, unit_rows, width), BF16),
        pltpu.VMEM((2, unit_rows, width), BF16),
        pltpu.SemaphoreType.DMA,
        pltpu.SemaphoreType.DMA((n_source,)),
    ]
    out_shape = [pltpu.VMEM(acc_shape, F32)]
    if last:
        out_shape += [jax.ShapeDtypeStruct((n_col, part_rows // (2 * n_col), supers * width), F32)] * 2
        out_shape.append(jax.ShapeDtypeStruct((supers, width, width), F32))
        scratch = [
            pltpu.VMEM((n_upper, size.main, 2, width, unit_rows), BF16),
            pltpu.VMEM((2, width, unit_rows), BF16),
            pltpu.SemaphoreType.DMA((n_upper,)),
        ] + scratch
    else:
        out_shape.append(jax.ShapeDtypeStruct((8, 128), F32))
    return pl.pallas_call(
        functools.partial(column_kernel, size, n_source, n_upper, len(after), part_rows, 2 * n_col, first, last),
        out_shape=out_shape,
        grid_spec=pltpu.PrefetchScalarGridSpec(
            num_scalar_prefetch=2,
            grid=(n_source * units,),
            in_specs=in_specs,
            out_specs=[whole_vmem()] * len(out_shape),
            scratch_shapes=scratch,
        ),
        input_output_aliases={} if first else {3: 0},
        compiler_params=params(),
        cost_estimate=cost(1000, 1000),
        name="column_phase",
    )(prefetch, slot, weights, *([] if first else [acc]), inverse, *flat, *after)


def body(inverse, lower, upper, diag_inverse, weights, pattern):
    n_row = lax.axis_size("row")
    n_col = lax.axis_size("col")
    n_pole = lax.axis_size("pole")
    assert n_pole == 2
    row_index = lax.axis_index("row")
    col_index = lax.axis_index("col")
    pole_index = lax.axis_index("pole")
    local_rows, _, supers, width = lower.shape[1:]
    inverse = inverse[0]
    part_rows, part_cols = inverse.shape[1:]
    unit_rows = min(width, local_rows)
    units = local_rows // unit_rows
    size = Sizes(units, supers, unit_rows, width)
    weight = weights[0]
    lower_from = [(row_index,)] + hop_sources(row_index, n_row)
    upper_from = [p for pair in hop_sources(col_index, n_col) for p in pair]

    slot, most = unit_tables(pattern, n_row * n_col, units, unit_rows, width)
    crowded = most > size.main
    row_slot = lax.dynamic_slice_in_dim(slot, row_index * n_col, n_col, 0).reshape(-1)
    col_slot = lax.dynamic_slice_in_dim(slot, col_index * n_row, n_row, 0).reshape(-1)
    lower_parts = jnp.transpose(lower[0], (1, 2, 0, 3))
    own_lower, spare_lower = pack(lower_parts, pick(slot, col_index * n_row + row_index), size, False)
    own_lower, spare_lower, upper = fence((own_lower, spare_lower, upper))
    upper_parts = jnp.transpose(upper[0], (1, 2, 0, 3))
    own_upper = pack(upper_parts, pick(slot, row_index * n_col + col_index), size, True)

    def first_part(size):
        def run(own_upper, own_lower, spare_lower):
            sums = row_product(inverse, None, col_index, pole_index, row_slot, weight, own_upper, size, tile, share)
            sums, own_lower = fence((sums, own_lower))
            pieces = [(own_lower, spare_lower)]
            acc, token = column_phase(inverse, None, [row_index], [], col_slot, weight, pieces, [], size, n_col)
            return sums, acc, token

        return run

    tile = min(1024, part_cols)
    share = part_cols // (n_row * n_pole)
    passing = hop((own_lower,), "row", n_row, 1)
    upper_got = [p for pair in line_gather(own_upper[0], "col", n_col) for p in pair]
    sums, acc, token = lax.cond(
        crowded, first_part(size), first_part(size.usual()), own_upper, own_lower, spare_lower
    )
    passing, own_upper, upper_got, sums, token = fence((passing, own_upper, upper_got, sums, token))

    def send(pieces):
        return jax.tree.leaves([line_gather(pieces[0], "row", n_row), line_gather(pieces[1], "col", n_col)])

    def skip(pieces):
        return list(blank(jax.eval_shape(send, pieces)))

    spread = lax.cond(crowded, send, skip, (spare_lower, own_upper[1]))
    row_spares, col_spares = spread[: len(spread) - len(upper_got)], spread[len(spread) - len(upper_got) :]
    uppers = [own_upper] + list(zip(upper_got, col_spares))

    def second_part(size):
        def run(sums, got, col_spares):
            for source, *pieces in zip(upper_from, got, col_spares):
                sums = row_product(inverse, sums, source, pole_index, row_slot, weight, pieces, size, tile, share)
            if len(sums) == 2:
                terms = (sums[0], swap(sums[1], "pole"))
            else:
                both = jnp.transpose(sums[0], (1, 0, 2)).reshape(supers * width, n_row, n_pole, share)
                both = jnp.transpose(both, (2, 1, 0, 3))
                terms = (pick(both, pole_index), swap(pick(both, 1 - pole_index), "pole"))
            return terms, scatter_codes(terms, (), "row", n_row, 0)

        return run

    held = [(1, passing)]
    if n_row > 2:
        passing = hop(passing, "row", n_row, 2)
    terms, codes = lax.cond(
        crowded, second_part(size), second_part(size.usual()), sums, upper_got, col_spares
    )
    carried = scatter_move(codes, "row", n_row, 0)
    passing, terms, carried = fence((passing, terms, carried))

    def spare_pair(t):
        return row_spares[(t - 1) * len(held[-1][1]) : t * len(held[-1][1])]

    def phase(acc, held, last):
        sources = [p for t, _ in held for p in lower_from[t]]
        pieces = [p for t, pair in held for p in zip(pair, spare_pair(t) if t else [spare_lower])]
        if not last:
            return column_phase(inverse, acc, sources, [], col_slot, weight, pieces, [], size, n_col)
        positions = [col_index] + upper_from + [pole_index]
        slots = jnp.concatenate([col_slot, row_slot])
        return column_phase(inverse, acc, sources, positions, slots, weight, pieces, uppers, size, n_col, (token,))

    stage = 1
    if stage < n_row - 1:
        codes = scatter_codes(terms, carried, "row", n_row, stage)
    for t in range(3, n_row):
        held.append((t - 1, passing))
        passing = hop(passing, "row", n_row, t)
        carried = scatter_move(codes, "row", n_row, stage)
        stage += 1
        if t == n_row - 1:
            acc, token = phase(acc, held, False)
            held = []
        codes = scatter_codes(terms, carried, "row", n_row, stage)
        passing, token, terms, codes = fence((passing, token, terms, codes))
    if n_row > 2:
        held.append((n_row - 1, passing))
    if stage < n_row - 1:
        carried = scatter_move(codes, "row", n_row, stage)
    _, keep, give, t_part = phase(acc, held, True)
    keep, give, t_part, terms, carried = fence((keep, give, t_part, terms, carried))

    col_terms = (keep, swap(give, "pole"))
    col_codes = scatter_codes(col_terms, (), "col", n_col, 0)

    given = diag_inverse[0].astype(F32)
    own_term = weight[0] * given[:, 1] + weight[1] * given[:, 0]
    owner = jnp.logical_and(row_index == 0, col_index == 0)
    t_part = (t_part + jnp.where(owner, own_term, 0.0)).reshape(n_pole, -1, width)
    t_sum = pick(t_part, pole_index) + swap(pick(t_part, 1 - pole_index), "pole")
    if n_col == 2:
        t_sum = t_sum.reshape(n_col, -1, width)
        t_sum = pick(t_sum, col_index) + swap(pick(t_sum, 1 - col_index), "col")
    else:
        t_sum = direct_sum(t_sum, "col", n_col)
    t_sum, col_codes = fence((t_sum, col_codes))
    for t in range(n_col - 1):
        col_carried = scatter_move(col_codes, "col", n_col, t)
        if t < n_col - 2:
            col_codes = scatter_codes(col_terms, col_carried, "col", n_col, t + 1)
    t_sum = direct_sum(t_sum, "row", n_row)
    row_density = finish(terms, row_index, carried, supers, width, True)
    t_sum, col_carried, row_density = fence((t_sum, col_carried, row_density))
    column_density = finish(col_terms, col_index, col_carried, supers, width, False)
    if n_col == 2:
        t_sum = halves_back(t_sum, "col", n_col)
    t_sum, column_density = fence((t_sum, column_density))
    diagonal_density = halves_back(t_sum, "pole", n_pole).reshape(supers, width, width)
    return (column_density, row_density, diagonal_density)


def solution(mesh):
    return jax.shard_map(
        body,
        mesh=mesh,
        in_specs=(
            P(("groups", "pole"), None, "row", "col"),
            P(("groups", "pole"), ("col", "row"), None, None, None),
            P(("groups", "pole"), ("row", "col"), None, None, None),
            P(("groups", "pole"), None, None, None, None),
            P(("groups", "pole"), None),
            P("groups", None),
        ),
        out_specs=(
            P(("groups", "row", "col", "pole"), None, None),
            P(("groups", "col", "row", "pole"), None, None),
            P("groups", None, None),
        ),
        check_vma=False,
    )
```

```python
import functools

import jax
import jax.numpy as jnp
from jax import lax
from jax.experimental import pallas as pl
from jax.experimental.pallas import tpu as pltpu
from jax.sharding import PartitionSpec as P

VMEM_LIMIT = 46 * 1024 * 1024
F32 = jnp.float32
BF16 = jnp.bfloat16


def params(limit=VMEM_LIMIT, **kw):
    return pltpu.CompilerParams(vmem_limit_bytes=limit, **kw)


def cost(flops, nbytes):
    return pl.CostEstimate(flops=int(flops), bytes_accessed=int(nbytes), transcendentals=0)


def fence(tree):
    return lax.optimization_barrier(tree)


def whole_vmem():
    return pl.BlockSpec(memory_space=pltpu.VMEM)


def smem():
    return pl.BlockSpec(memory_space=pltpu.SMEM)


def unit_tables(pattern, shards, units, unit_rows, width):
    supers = pattern.shape[0]
    block = (lax.iota(jnp.int32, shards * units) * unit_rows) // width
    hits = jnp.any(pattern[:, :, None] == block[None, None, :], axis=1)
    flags = jnp.transpose(hits).reshape(shards, units * supers).astype(jnp.int32)
    places = lax.iota(jnp.int32, units * supers)
    before = (places[:, None] < places[None, :]).astype(jnp.int32)
    rank = jnp.sum(flags[:, :, None] * before[None], axis=1)
    slot = jnp.where(flags > 0, rank, -1)
    most = jnp.max(jnp.sum(flags, axis=1))
    return slot, most


class Sizes:
    def __init__(self, units, supers, unit_rows, width):
        self.units, self.supers, self.unit_rows, self.width = units, supers, unit_rows, width
        self.main = units * max(supers - 1, 1)
        self.spare = units * supers - self.main

    def usual(self):
        size = Sizes(self.units, self.supers, self.unit_rows, self.width)
        size.spare = 0
        return size


def any_space():
    return pl.BlockSpec(memory_space=pl.ANY)


def pack_kernel(size, transposed, slot_ref, x_ref, main_ref, spare_ref):
    rows = size.unit_rows
    for u in range(size.units):
        for s in range(size.supers):
            slot = slot_ref[u * size.supers + s]

            def store(ref, at):
                for h in range(2):
                    tile = x_ref[h, s, u * rows : (u + 1) * rows, :]
                    ref[at, h] = tile.T if transposed else tile

            @pl.when(jnp.logical_and(slot >= 0, slot < size.main))
            def _():
                store(main_ref, slot)

            if size.spare:

                @pl.when(slot >= size.main)
                def _():
                    store(spare_ref, slot - size.main)


def pack(x, slot, size, transposed):
    tile = (2, size.width, size.unit_rows) if transposed else (2, size.unit_rows, size.width)
    return pl.pallas_call(
        functools.partial(pack_kernel, size, transposed),
        out_shape=[
            jax.ShapeDtypeStruct((size.main,) + tile, x.dtype),
            jax.ShapeDtypeStruct((max(size.units * size.supers - size.main, 1),) + tile, x.dtype),
        ],
        in_specs=[smem(), whole_vmem()],
        out_specs=[whole_vmem()] * 2,
        compiler_params=params(),
        cost_estimate=cost(1000, 1000),
        name="pack",
    )(slot, x)


def blank(like):
    return pl.pallas_call(
        lambda *refs: None,
        out_shape=tuple(like),
        out_specs=[any_space()] * len(like),
        compiler_params=params(has_side_effects=True),
        name="blank",
    )()


def swap(x, axis):
    return lax.ppermute(x, axis, [(0, 1), (1, 0)])


def hop(pair, axis, n, t):
    if n == 2:
        return (swap(pair[0], axis),)
    right = lax.ppermute(pair[0], axis, [(i, i + 1) for i in range(t - 1, n - 1)])
    left = lax.ppermute(pair[-1], axis, [(i + 1, i) for i in range(0, n - t)])
    return (right, left)


def line_gather(x, axis, n):
    hops = [(x,)]
    for t in range(1, n):
        hops.append(hop(hops[-1], axis, n, t))
    return hops[1:]


def hop_sources(index, n):
    if n == 2:
        return [(1 - index,)]
    return [
        (jnp.where(index - t >= 0, index - t, -1), jnp.where(index + t < n, index + t, -1)) for t in range(1, n)
    ]


def pick(shards, d):
    return lax.dynamic_index_in_dim(shards, d, 0, keepdims=False)


CODE_ROWS = 16


def decoded(codes, exponents):
    return codes.astype(jnp.int32).astype(F32) * jnp.exp2(exponents[:1].astype(jnp.int32).astype(F32))


def shard_specs(terms, shape, place):
    return [pl.BlockSpec((1,) + shape, lambda j, at: (at[0],) + place(j))] * len(terms)


def term_sum(n_term, refs):
    return functools.reduce(jnp.add, [ref[0] for ref in refs[:n_term]]), refs[n_term:]


def pick_kernel(n_term, rows, index_ref, *refs):
    total, refs = term_sum(n_term, refs)
    for ref in refs[:-1]:
        total = total + decoded(ref[:rows, :], ref[rows:, :])
    out = refs[-1]
    most = jnp.maximum(jnp.max(jnp.abs(total), axis=0, keepdims=True), 1e-30)
    exponent = jnp.ceil(jnp.log2(most) + 0.01) - 15.0
    codes = jnp.floor(total / jnp.exp2(exponent) + 0.5)
    out[:rows, :] = jnp.clip(codes, -32767.0, 32767.0).astype(jnp.int32).astype(jnp.int16)
    out[rows:, :] = jnp.broadcast_to(exponent, (CODE_ROWS, exponent.shape[1])).astype(jnp.int32).astype(jnp.int16)


def pick_coded(terms, d, extra=()):
    rows, w = terms[0].shape[1:]
    step = 256 if w % 256 == 0 else w
    coded = pl.BlockSpec((rows + CODE_ROWS, step), lambda j, at: (0, j))
    return pl.pallas_call(
        functools.partial(pick_kernel, len(terms), rows),
        out_shape=jax.ShapeDtypeStruct((rows + CODE_ROWS, w), jnp.int16),
        grid_spec=pltpu.PrefetchScalarGridSpec(
            num_scalar_prefetch=1,
            grid=(w // step,),
            in_specs=shard_specs(terms, (rows, step), lambda j: (0, j)) + [coded] * len(extra),
            out_specs=coded,
        ),
        compiler_params=params(),
        cost_estimate=cost(1000, 1000),
        name="pick_coded",
    )(jnp.asarray(d, jnp.int32).reshape(1), *terms, *extra)


def finish_kernel(n_term, transposed, index_ref, *refs):
    total, refs = term_sum(n_term, refs)
    coded = refs[:-1]
    for codes, exponents in zip(coded[::2], coded[1::2]):
        total = total + decoded(codes[...], exponents[...])
    refs[-1][0] = total.T if transposed else total


def finish(terms, d, extra, supers, width, transposed):
    rows, w = terms[0].shape[1:]
    share = w if transposed else rows
    tall = rows // CODE_ROWS
    if transposed:
        term = shard_specs(terms, (width, w), lambda s: (s, 0))
        codes = pl.BlockSpec((width, w), lambda s, at: (s, 0))
        exponents = pl.BlockSpec((CODE_ROWS, w), lambda s, at: (tall, 0))
    else:
        term = shard_specs(terms, (rows, width), lambda s: (0, s))
        codes = pl.BlockSpec((rows, width), lambda s, at: (0, s))
        exponents = pl.BlockSpec((CODE_ROWS, width), lambda s, at: (tall, s))
    total = pl.pallas_call(
        functools.partial(finish_kernel, len(terms), transposed),
        out_shape=jax.ShapeDtypeStruct((supers, share, width), F32),
        grid_spec=pltpu.PrefetchScalarGridSpec(
            num_scalar_prefetch=1,
            grid=(supers,),
            in_specs=term + [codes, exponents] * len(extra),
            out_specs=pl.BlockSpec((1, share, width), lambda s, at: (s, 0, 0)),
        ),
        compiler_params=params(),
        cost_estimate=cost(1000, 1000),
        name="finish",
    )(jnp.asarray(d, jnp.int32).reshape(1), *terms, *[x for x in extra for _ in range(2)])
    return jnp.transpose(total, (1, 0, 2))


def scatter_codes(terms, carried, axis, n, t):
    i = lax.axis_index(axis)
    if n == 2:
        return (pick_coded(terms, 1 - i),)
    right = pick_coded(terms, jnp.clip(n - 1 - t + i, 0, n - 1), carried[:1])
    left = pick_coded(terms, jnp.clip(t - (n - 1 - i), 0, n - 1), carried[1:])
    return (right, left)


def scatter_move(codes, axis, n, t):
    if n == 2:
        return (swap(codes[0], axis),)
    right = lax.ppermute(codes[0], axis, [(j, j + 1) for j in range(t + 1)])
    left = lax.ppermute(codes[1], axis, [(n - 1 - j, n - 2 - j) for j in range(t + 1)])
    return (right, left)


def direct_sum(x, axis, n):
    if n & (n - 1):
        return lax.psum(x, axis)
    k = 1
    while k < n:
        x = x + lax.ppermute(x, axis, [(j, j ^ k) for j in range(n)])
        k *= 2
    return x


def halves_back(x, axis, n):
    if n != 2:
        return lax.all_gather(x, axis, axis=0, tiled=True)
    other = lax.ppermute(x, axis, [(0, 1), (1, 0)])
    swap = lax.axis_index(axis) == 1
    return jnp.concatenate([jnp.where(swap, other, x), jnp.where(swap, x, other)])


def with_unit(size, main_ref, spare_ref, buffer, sem, slot, use):
    @pl.when(jnp.logical_and(slot >= 0, slot < size.main))
    def _():
        use(main_ref[slot, 0], main_ref[slot, 1])

    if size.spare:
        with_spare(size, spare_ref, buffer, sem, slot, use)


def with_spare(size, spare_ref, buffer, sem, slot, use):
    @pl.when(slot >= size.main)
    def _():
        copy = pltpu.make_async_copy(spare_ref.at[slot - size.main], buffer, sem)
        copy.start()
        copy.wait()
        use(buffer[0], buffer[1])


def row_kernel(size, first, paired, share, source_ref, slot_ref, weight_ref, *refs):
    refs = list(refs)
    a_ref, main_ref, spare_ref = refs[:3]
    refs = refs[3:]
    n_out = 2 if paired else 1
    before = None if first else refs[:n_out]
    refs = refs[0 if first else n_out :]
    outs, (left, kept, buffer, sem) = refs[:n_out], refs[n_out:]
    units, supers, half, unit_rows = size.units, size.supers, size.width, size.unit_rows
    deep = 2 * unit_rows
    shard = source_ref[0]

    @pl.when(pl.program_id(0) == 0)
    def _():
        for s in range(supers):
            kept[s, units] = 0
            for u in range(units):
                slot = jnp.where(shard >= 0, slot_ref[(jnp.maximum(shard, 0) * units + u) * supers + s], -1)

                def build(real, imag, s=s, u=u):
                    at = kept[s, units]
                    left[s, at, :half, :unit_rows] = real
                    left[s, at, :half, unit_rows:] = -imag
                    left[s, at, half:, :unit_rows] = imag
                    left[s, at, half:, unit_rows:] = real
                    kept[s, at] = u
                    kept[s, units] = at + 1

                with_unit(size, main_ref, spare_ref, buffer, sem, slot, build)

    pole = source_ref[1]

    def store(s, mix):
        rows = pl.ds(pl.multiple_of(s * half, half), half)
        for part in range(2 if paired else 1):
            value = mix[:, part * share : (part + 1) * share] if paired else mix

            def put(out, old):
                if old is None:
                    out[0, rows, :] = -value
                else:
                    out[0, rows, :] = old[0, rows, :] - value

            if not paired:
                put(outs[0], None if first else before[0])
                continue

            @pl.when(pole == part)
            def _():
                put(outs[0], None if first else before[0])

            @pl.when(pole != part)
            def _():
                put(outs[1], None if first else before[1])

    def one(s, _):
        count = kept[s, units]

        @pl.when(count == 0)
        def _():
            store(s, jnp.zeros((half, a_ref.shape[2]), F32))

        for many in range(1, units + 1):

            @pl.when(count == many)
            def _():
                tall = []
                wide = []
                for i in range(many):
                    rows = pl.ds(pl.multiple_of(kept[s, i] * unit_rows, unit_rows), unit_rows)
                    tall += [a_ref[0, rows, :], a_ref[1, rows, :]]
                    wide.append(left[s, i])
                wide = wide[0] if many == 1 else jnp.concatenate(wide, axis=1)
                sums = jnp.dot(wide, jnp.concatenate(tall, axis=0), preferred_element_type=F32)
                store(s, weight_ref[1] * sums[:half] + weight_ref[0] * sums[half:])

        return 0

    lax.fori_loop(0, supers, one, 0)


def row_product(inverse, before, source, pole, slot, weights, pieces, size, tile, share):
    first = before is None
    part_rows, part_cols = inverse.shape[1:]
    rows = size.units * size.unit_rows
    deep = size.supers * size.width
    count = part_cols // tile
    paired = tile == 2 * share
    thin = share if paired else tile
    n_out = 2 if paired else 1
    tiles = [pl.BlockSpec((1, deep, thin), lambda j, *_: (j, 0, 0))] * n_out
    outs = [jax.ShapeDtypeStruct((count, deep, thin), F32)] * n_out
    return pl.pallas_call(
        functools.partial(row_kernel, size, first, paired, share),
        out_shape=outs,
        grid_spec=pltpu.PrefetchScalarGridSpec(
            num_scalar_prefetch=2,
            grid=(count,),
            in_specs=[smem(), pl.BlockSpec((2, rows, tile), lambda j, src, _: (0, jnp.maximum(src[0], 0), j))]
            + [whole_vmem(), any_space()]
            + ([] if first else tiles),
            out_specs=tiles,
            scratch_shapes=[
                pltpu.VMEM((size.supers, size.units, 2 * size.width, 2 * size.unit_rows), BF16),
                pltpu.SMEM((size.supers, size.units + 1), jnp.int32),
                pltpu.VMEM((2, size.width, size.unit_rows), BF16),
                pltpu.SemaphoreType.DMA,
            ],
        ),
        compiler_params=params(),
        cost_estimate=cost(1000, 1000),
        name="row_product",
    )(jnp.stack([source, pole]), slot, weights, inverse, *pieces, *([] if first else before))


def column_kernel(size, n_source, n_upper, n_after, part_rows, n_share, first, last, source_ref, slot_ref, weight_ref, *refs):
    units, supers, width, unit_rows = size.units, size.supers, size.width, size.unit_rows
    refs = list(refs)
    acc_in = None if first else refs.pop(0)
    given_ref = refs.pop(0) if last else None
    a_ref = refs.pop(0)
    pieces = [(refs.pop(0), refs.pop(0)) for _ in range(n_source)]
    uppers = [(refs.pop(0), refs.pop(0)) for _ in range(n_upper)]
    refs = refs[n_after:]
    if last:
        keep_out, send_out, t_ref = refs[:3]
        keep_ref, send_ref, x_sems, upper_mains, upper_buffer, upper_sems = refs[3:9]
        refs = refs[9:]
    else:
        acc_out, token_ref = refs.pop(0), refs.pop(0)
    acc, right, mains, buffer, sem, main_sems, acc_sems = refs
    step = pl.program_id(0)
    loads = [pltpu.make_async_copy(pieces[q][0], mains.at[q], main_sems.at[q]) for q in range(n_source)]
    acc_loads = []
    if not first:
        acc_loads = [pltpu.make_async_copy(acc_in.at[s], acc.at[s], acc_sems.at[s]) for s in range(supers)]
    acc_stores = []
    if not last:
        acc_stores = [pltpu.make_async_copy(acc.at[s], acc_out.at[s], acc_sems.at[s]) for s in range(supers)]
    upper_loads = [pltpu.make_async_copy(uppers[q][0], upper_mains.at[q], upper_sems.at[q]) for q in range(n_upper)]

    @pl.when(step == 0)
    def _():
        for load in loads[:1] + acc_loads + loads[1:] + upper_loads:
            load.start()
        if not last:
            token_ref[...] = jnp.zeros_like(token_ref)
        if first:
            acc[...] = jnp.zeros_like(acc)

    for q in range(n_source):

        @pl.when(step == q * units)
        def _():
            loads[q].wait()

    source = step // units
    shard = source_ref[source]
    place = jnp.maximum(shard, 0) * units + step % units

    for s in range(supers):
        slot = jnp.where(shard >= 0, slot_ref[place * supers + s], -1)

        def build(real, imag):
            right[:unit_rows, :width] = real
            right[:unit_rows, width:] = imag
            right[unit_rows:, :width] = -imag
            right[unit_rows:, width:] = real

        @pl.when(jnp.logical_and(slot >= 0, slot < size.main))
        def _():
            build(mains[source, slot, 0], mains[source, slot, 1])

        if size.spare:
            for q in range(n_source):
                with_spare(size, pieces[q][1], buffer, sem, jnp.where(source == q, slot, -1), build)

        if not first:

            @pl.when(step == 0)
            def _():
                acc_loads[s].wait()

        @pl.when(slot >= 0)
        def _():
            both = jnp.concatenate([a_ref[0], a_ref[1]], axis=1)
            acc[s] += jnp.dot(both, right[...], preferred_element_type=F32)

        if not last:

            @pl.when(step == n_source * units - 1)
            def _():
                acc_stores[s].start()

    if not last:

        @pl.when(step == n_source * units - 1)
        def _():
            for store in acc_stores:
                store.wait()

        return

    @pl.when(step == n_source * units - 1)
    def _():
        weight_real = weight_ref[0]
        weight_imag = weight_ref[1]
        pole = source_ref[n_source + n_upper]
        share = part_rows // n_share
        for load in upper_loads:
            load.wait()
        for k in range(n_share):
            rows = slice(k * share, (k + 1) * share)
            for part, out in ((0, keep_ref), (1, send_ref)):

                @pl.when((pole == k % 2) == (part == 0))
                def _():
                    for s in range(supers):
                        out[k // 2, :, s * width : (s + 1) * width] = -(
                            weight_imag * acc[s, rows, :width] + weight_real * acc[s, rows, width:]
                        )

        x_stores = [
            pltpu.make_async_copy(keep_ref, keep_out, x_sems.at[0]),
            pltpu.make_async_copy(send_ref, send_out, x_sems.at[1]),
        ]
        for store in x_stores:
            store.start()

        t_ref[...] = given_ref[...]

        def unit(k, _):
            rows = pl.ds(pl.multiple_of(k * unit_rows, unit_rows), unit_rows)
            upper = jnp.int32(0)
            for q in range(n_upper):
                upper = jnp.where(source_ref[n_source + q] == k // units, q, upper)
            for s in range(supers):
                slot = slot_ref[n_slots + k * supers + s]

                def use(real, imag):
                    first_acc = acc[s, rows, :width]
                    second_acc = acc[s, rows, width:]
                    mix = weight_imag * first_acc + weight_real * second_acc
                    other = weight_real * first_acc - weight_imag * second_acc
                    stacked = jnp.concatenate([mix, other], axis=0)
                    high = stacked.astype(BF16)
                    low = (stacked - high.astype(F32)).astype(BF16)
                    both = jnp.concatenate([real, imag], axis=1)
                    sums = jnp.dot(both, jnp.concatenate([high, low], axis=1), preferred_element_type=F32)
                    t_ref[s] += sums[:, :width] + sums[:, width:]

                @pl.when(jnp.logical_and(slot >= 0, slot < size.main))
                def _():
                    use(upper_mains[upper, slot, 0], upper_mains[upper, slot, 1])

                if size.spare:
                    for q in range(n_upper):
                        with_spare(size, uppers[q][1], upper_buffer, sem, jnp.where(upper == q, slot, -1), use)

            return 0

        n_slots = slot_ref.shape[0] - part_rows // unit_rows * supers
        lax.fori_loop(0, part_rows // unit_rows, unit, 0)
        for store in x_stores:
            store.wait()


def column_phase(inverse, acc, sources, positions, slot, weights, pieces, uppers, size, n_col, given=(), after=()):
    first, last = acc is None, bool(uppers)
    n_source, n_upper = len(pieces), len(uppers)
    part_rows, part_cols = inverse.shape[1:]
    units, unit_rows, supers, width = size.units, size.unit_rows, size.supers, size.width
    flat = [p for group in pieces + uppers for p in group]

    steps = []
    for q in range(n_source):
        idle = jnp.int32(0)
        for other in [*range(n_source - 1, q, -1), *range(q)]:
            edge = sources[other] * units + (units - 1 if other < q else 0)
            idle = jnp.where(sources[other] >= 0, edge, idle)
        steps.append(jnp.where(sources[q] >= 0, sources[q] * units + lax.iota(jnp.int32, units), idle))
    prefetch = jnp.concatenate([jnp.stack(sources + positions)] + steps)

    def a_map(g, src, _):
        return (0, 0, src[len(sources) + len(positions) + g])

    acc_shape = (supers, part_rows, 2 * width)
    in_specs = [smem()] + ([] if first else [any_space()]) + ([whole_vmem()] if last else [])
    in_specs += [pl.BlockSpec((2, part_rows, unit_rows), a_map)] + [any_space()] * (len(flat) + len(after))
    scratch = [
        pltpu.VMEM((2 * unit_rows, 2 * width), BF16),
        pltpu.VMEM((n_source, size.main, 2, unit_rows, width), BF16),
        pltpu.VMEM((2, unit_rows, width), BF16),
        pltpu.SemaphoreType.DMA,
        pltpu.SemaphoreType.DMA((n_source,)),
        pltpu.SemaphoreType.DMA((supers,)),
    ]
    scratch.insert(0, pltpu.VMEM(acc_shape, F32))
    if last:
        out_shape = [jax.ShapeDtypeStruct((n_col, part_rows // (2 * n_col), supers * width), F32)] * 2
        out_shape.append(jax.ShapeDtypeStruct((supers, width, width), F32))
        scratch = [
            pltpu.VMEM(out_shape[0].shape, F32),
            pltpu.VMEM(out_shape[0].shape, F32),
            pltpu.SemaphoreType.DMA((2,)),
            pltpu.VMEM((n_upper, size.main, 2, width, unit_rows), BF16),
            pltpu.VMEM((2, width, unit_rows), BF16),
            pltpu.SemaphoreType.DMA((n_upper,)),
        ] + scratch
        out_specs = [any_space(), any_space(), whole_vmem()]
    else:
        out_shape = [jax.ShapeDtypeStruct(acc_shape, F32), jax.ShapeDtypeStruct((8, 128), F32)]
        out_specs = [any_space(), whole_vmem()]
    return pl.pallas_call(
        functools.partial(column_kernel, size, n_source, n_upper, len(after), part_rows, 2 * n_col, first, last),
        out_shape=out_shape,
        grid_spec=pltpu.PrefetchScalarGridSpec(
            num_scalar_prefetch=2,
            grid=(n_source * units,),
            in_specs=in_specs,
            out_specs=out_specs,
            scratch_shapes=scratch,
        ),
        compiler_params=params(),
        cost_estimate=cost(1000, 1000),
        name="column_phase",
    )(prefetch, slot, weights, *([] if first else [acc]), *given, inverse, *flat, *after)


def body(inverse, lower, upper, diag_inverse, weights, pattern):
    n_row = lax.axis_size("row")
    n_col = lax.axis_size("col")
    n_pole = lax.axis_size("pole")
    assert n_pole == 2
    row_index = lax.axis_index("row")
    col_index = lax.axis_index("col")
    pole_index = lax.axis_index("pole")
    local_rows, _, supers, width = lower.shape[1:]
    inverse = inverse[0]
    part_rows, part_cols = inverse.shape[1:]
    unit_rows = min(width, local_rows)
    units = local_rows // unit_rows
    size = Sizes(units, supers, unit_rows, width)
    weight = weights[0]
    lower_from = [(row_index,)] + hop_sources(row_index, n_row)
    upper_from = [p for pair in hop_sources(col_index, n_col) for p in pair]

    slot, most = unit_tables(pattern, n_row * n_col, units, unit_rows, width)
    crowded = most > size.main
    row_slot = lax.dynamic_slice_in_dim(slot, row_index * n_col, n_col, 0).reshape(-1)
    col_slot = lax.dynamic_slice_in_dim(slot, col_index * n_row, n_row, 0).reshape(-1)
    lower_parts = jnp.transpose(lower[0], (1, 2, 0, 3))
    own_lower, spare_lower = pack(lower_parts, pick(slot, col_index * n_row + row_index), size, False)
    own_lower, spare_lower, upper = fence((own_lower, spare_lower, upper))
    upper_parts = jnp.transpose(upper[0], (1, 2, 0, 3))
    own_upper = pack(upper_parts, pick(slot, row_index * n_col + col_index), size, True)

    def first_part(size):
        def run(own_upper, own_lower, spare_lower):
            sums = row_product(inverse, None, col_index, pole_index, row_slot, weight, own_upper, size, tile, share)
            sums, own_lower = fence((sums, own_lower))
            pieces = [(own_lower, spare_lower)]
            acc, token = column_phase(inverse, None, [row_index], [], col_slot, weight, pieces, [], size, n_col)
            return sums, acc, token

        return run

    given = diag_inverse[0].astype(F32)
    own_term = weight[0] * given[:, 1] + weight[1] * given[:, 0]
    owner = jnp.logical_and(row_index == 0, col_index == 0)
    own_term = jnp.where(owner, own_term, 0.0)

    tile = min(1024, part_cols)
    share = part_cols // (n_row * n_pole)
    passing = hop((own_lower,), "row", n_row, 1)
    upper_got = [p for pair in line_gather(own_upper[0], "col", n_col) for p in pair]
    sums, acc, token = lax.cond(
        crowded, first_part(size), first_part(size.usual()), own_upper, own_lower, spare_lower
    )
    passing, own_upper, upper_got, sums, token, own_term = fence(
        (passing, own_upper, upper_got, sums, token, own_term)
    )

    def send(pieces):
        return jax.tree.leaves([line_gather(pieces[0], "row", n_row), line_gather(pieces[1], "col", n_col)])

    def skip(pieces):
        return list(blank(jax.eval_shape(send, pieces)))

    spread = lax.cond(crowded, send, skip, (spare_lower, own_upper[1]))
    row_spares, col_spares = spread[: len(spread) - len(upper_got)], spread[len(spread) - len(upper_got) :]
    uppers = [own_upper] + list(zip(upper_got, col_spares))

    def second_part(size):
        def run(sums, got, col_spares):
            for source, *pieces in zip(upper_from, got, col_spares):
                sums = row_product(inverse, sums, source, pole_index, row_slot, weight, pieces, size, tile, share)
            if len(sums) == 2:
                terms = (sums[0], swap(sums[1], "pole"))
            else:
                both = jnp.transpose(sums[0], (1, 0, 2)).reshape(supers * width, n_row, n_pole, share)
                both = jnp.transpose(both, (2, 1, 0, 3))
                terms = (pick(both, pole_index), swap(pick(both, 1 - pole_index), "pole"))
            return terms, scatter_codes(terms, (), "row", n_row, 0)

        return run

    held = [(1, passing)]
    if n_row > 2:
        passing = hop(passing, "row", n_row, 2)
    terms, codes = lax.cond(
        crowded, second_part(size), second_part(size.usual()), sums, upper_got, col_spares
    )
    passing, terms, codes = fence((passing, terms, codes))

    def spare_pair(t):
        return row_spares[(t - 1) * len(held[-1][1]) : t * len(held[-1][1])]

    def phase(acc, held, last):
        sources = [p for t, _ in held for p in lower_from[t]]
        pieces = [p for t, pair in held for p in zip(pair, spare_pair(t) if t else [spare_lower])]
        if not last:
            return column_phase(inverse, acc, sources, [], col_slot, weight, pieces, [], size, n_col)
        positions = [col_index] + upper_from + [pole_index]
        slots = jnp.concatenate([col_slot, row_slot])
        return column_phase(
            inverse, acc, sources, positions, slots, weight, pieces, uppers, size, n_col, (own_term,), (token,)
        )

    stage = 0
    carried = ()
    for t in range(3, n_row):
        held.append((t - 1, passing))
        passing = hop(passing, "row", n_row, t)
        carried = scatter_move(codes, "row", n_row, stage)
        stage += 1
        if t == n_row - 1:
            acc, token = phase(acc, held, False)
            held = []
        codes = scatter_codes(terms, carried, "row", n_row, stage)
        passing, token, terms, codes = fence((passing, token, terms, codes))
    if n_row > 2:
        held.append((n_row - 1, passing))
        carried = scatter_move(codes, "row", n_row, stage)
        stage += 1
    keep, give, t_part = phase(acc, held, True)
    keep, give, t_part, terms, carried, codes = fence((keep, give, t_part, terms, carried, codes))
    if n_row > 2:
        codes = scatter_codes(terms, carried, "row", n_row, stage)

    carried = scatter_move(codes, "row", n_row, stage)
    col_terms = (keep, swap(give, "pole"))
    col_codes = scatter_codes(col_terms, (), "col", n_col, 0)

    t_part = t_part.reshape(n_pole, -1, width)
    t_sum = pick(t_part, pole_index) + swap(pick(t_part, 1 - pole_index), "pole")
    if n_col == 2:
        t_sum = t_sum.reshape(n_col, -1, width)
        t_sum = pick(t_sum, col_index) + swap(pick(t_sum, 1 - col_index), "col")
    else:
        t_sum = direct_sum(t_sum, "col", n_col)
    t_sum, col_codes, carried = fence((t_sum, col_codes, carried))
    for t in range(n_col - 1):
        col_carried = scatter_move(col_codes, "col", n_col, t)
        if t < n_col - 2:
            col_codes = scatter_codes(col_terms, col_carried, "col", n_col, t + 1)
    t_sum = direct_sum(t_sum, "row", n_row)
    row_density = finish(terms, row_index, carried, supers, width, True)
    t_sum, col_carried, row_density = fence((t_sum, col_carried, row_density))
    column_density = finish(col_terms, col_index, col_carried, supers, width, False)
    if n_col == 2:
        t_sum = halves_back(t_sum, "col", n_col)
    t_sum, column_density = fence((t_sum, column_density))
    diagonal_density = halves_back(t_sum, "pole", n_pole).reshape(supers, width, width)
    return (column_density, row_density, diagonal_density)


def solution(mesh):
    return jax.shard_map(
        body,
        mesh=mesh,
        in_specs=(
            P(("groups", "pole"), None, "row", "col"),
            P(("groups", "pole"), ("col", "row"), None, None, None),
            P(("groups", "pole"), ("row", "col"), None, None, None),
            P(("groups", "pole"), None, None, None, None),
            P(("groups", "pole"), None),
            P("groups", None),
        ),
        out_specs=(
            P(("groups", "row", "col", "pole"), None, None),
            P(("groups", "col", "row", "pole"), None, None),
            P("groups", None, None),
        ),
        check_vma=False,
    )
```

```python
import functools

import jax
import jax.numpy as jnp
from jax import lax
from jax.experimental import pallas as pl
from jax.experimental.pallas import tpu as pltpu
from jax.sharding import PartitionSpec as P

VMEM_LIMIT = 46 * 1024 * 1024
F32 = jnp.float32
BF16 = jnp.bfloat16


def params(limit=VMEM_LIMIT, **kw):
    return pltpu.CompilerParams(vmem_limit_bytes=limit, **kw)


def cost(flops, nbytes):
    return pl.CostEstimate(flops=int(flops), bytes_accessed=int(nbytes), transcendentals=0)


def fence(tree):
    return lax.optimization_barrier(tree)


def whole_vmem():
    return pl.BlockSpec(memory_space=pltpu.VMEM)


def smem():
    return pl.BlockSpec(memory_space=pltpu.SMEM)


def unit_tables(pattern, shards, units, unit_rows, width):
    supers = pattern.shape[0]
    block = (lax.iota(jnp.int32, shards * units) * unit_rows) // width
    hits = jnp.any(pattern[:, :, None] == block[None, None, :], axis=1)
    flags = jnp.transpose(hits).reshape(shards, units * supers).astype(jnp.int32)
    places = lax.iota(jnp.int32, units * supers)
    before = (places[:, None] < places[None, :]).astype(jnp.int32)
    rank = jnp.sum(flags[:, :, None] * before[None], axis=1)
    slot = jnp.where(flags > 0, rank, -1)
    most = jnp.max(jnp.sum(flags, axis=1))
    return slot, most


class Sizes:
    def __init__(self, units, supers, unit_rows, width):
        self.units, self.supers, self.unit_rows, self.width = units, supers, unit_rows, width
        self.main = units * max(supers - 1, 1)
        self.spare = units * supers - self.main

    def usual(self):
        size = Sizes(self.units, self.supers, self.unit_rows, self.width)
        size.spare = 0
        return size


def any_space():
    return pl.BlockSpec(memory_space=pl.ANY)


def pack_kernel(size, transposed, slot_ref, x_ref, main_ref, spare_ref):
    rows = size.unit_rows
    for u in range(size.units):
        for s in range(size.supers):
            slot = slot_ref[u * size.supers + s]

            def store(ref, at):
                for h in range(2):
                    tile = x_ref[h, s, u * rows : (u + 1) * rows, :]
                    ref[at, h] = tile.T if transposed else tile

            @pl.when(jnp.logical_and(slot >= 0, slot < size.main))
            def _():
                store(main_ref, slot)

            if size.spare:

                @pl.when(slot >= size.main)
                def _():
                    store(spare_ref, slot - size.main)


def pack(x, slot, size, transposed):
    tile = (2, size.width, size.unit_rows) if transposed else (2, size.unit_rows, size.width)
    return pl.pallas_call(
        functools.partial(pack_kernel, size, transposed),
        out_shape=[
            jax.ShapeDtypeStruct((size.main,) + tile, x.dtype),
            jax.ShapeDtypeStruct((max(size.units * size.supers - size.main, 1),) + tile, x.dtype),
        ],
        in_specs=[smem(), whole_vmem()],
        out_specs=[whole_vmem()] * 2,
        compiler_params=params(),
        cost_estimate=cost(1000, 1000),
        name="pack",
    )(slot, x)


def blank(like):
    return pl.pallas_call(
        lambda *refs: None,
        out_shape=tuple(like),
        out_specs=[any_space()] * len(like),
        compiler_params=params(has_side_effects=True),
        name="blank",
    )()


def swap(x, axis):
    return lax.ppermute(x, axis, [(0, 1), (1, 0)])


def hop(pair, axis, n, t):
    if n == 2:
        return (swap(pair[0], axis),)
    right = lax.ppermute(pair[0], axis, [(i, i + 1) for i in range(t - 1, n - 1)])
    left = lax.ppermute(pair[-1], axis, [(i + 1, i) for i in range(0, n - t)])
    return (right, left)


def line_gather(x, axis, n):
    hops = [(x,)]
    for t in range(1, n):
        hops.append(hop(hops[-1], axis, n, t))
    return hops[1:]


def hop_sources(index, n):
    if n == 2:
        return [(1 - index,)]
    return [
        (jnp.where(index - t >= 0, index - t, -1), jnp.where(index + t < n, index + t, -1)) for t in range(1, n)
    ]


def pick(shards, d):
    return lax.dynamic_index_in_dim(shards, d, 0, keepdims=False)


CODE_ROWS = 16


def decoded(codes, exponents):
    return codes.astype(jnp.int32).astype(F32) * jnp.exp2(exponents[:1].astype(jnp.int32).astype(F32))


def shard_specs(terms, shape, place):
    return [pl.BlockSpec((1,) + shape, lambda j, at: (at[0],) + place(j))] * len(terms)


def term_sum(n_term, refs):
    return functools.reduce(jnp.add, [ref[0] for ref in refs[:n_term]]), refs[n_term:]


def encode(total, out):
    rows = total.shape[0]
    most = jnp.maximum(jnp.max(jnp.abs(total), axis=0, keepdims=True), 1e-30)
    exponent = jnp.ceil(jnp.log2(most) + 0.01) - 15.0
    codes = jnp.floor(total * jnp.exp2(-exponent) + 0.5)
    out[:rows, :] = codes.astype(jnp.int32).astype(jnp.int16)
    out[rows:, :] = jnp.broadcast_to(exponent, (CODE_ROWS, exponent.shape[1])).astype(jnp.int32).astype(jnp.int16)


def pick_kernel(n_term, n_way, rows, index_ref, *refs):
    total, refs = term_sum(n_term, refs)
    extras, outs = refs[:-n_way], refs[-n_way:]
    for way in range(n_way):

        @pl.when(pl.program_id(0) == way)
        def _():
            mine = total
            if extras:
                mine = mine + decoded(extras[way][:rows, :], extras[way][rows:, :])
            encode(mine, outs[way])


def pick_coded(terms, shards, extra=()):
    rows, w = terms[0].shape[1:]
    step = 256 if w % 256 == 0 else w
    steps = w // step
    n_way = len(shards)

    def coded(way):
        def place(g, j, at):
            return (0, jnp.where(g == way, j, jnp.where(g < way, 0, steps - 1)))

        return pl.BlockSpec((rows + CODE_ROWS, step), place)

    ways = [coded(way) for way in range(n_way)]
    return pl.pallas_call(
        functools.partial(pick_kernel, len(terms), n_way, rows),
        out_shape=[jax.ShapeDtypeStruct((rows + CODE_ROWS, w), jnp.int16)] * n_way,
        grid_spec=pltpu.PrefetchScalarGridSpec(
            num_scalar_prefetch=1,
            grid=(n_way, steps),
            in_specs=[pl.BlockSpec((1, rows, step), lambda g, j, at: (at[g], 0, j))] * len(terms)
            + (ways if extra else []),
            out_specs=ways,
        ),
        compiler_params=params(),
        cost_estimate=cost(1000, 1000),
        name="pick_coded",
    )(jnp.stack(shards).astype(jnp.int32), *terms, *extra)


def finish_kernel(n_term, transposed, index_ref, *refs):
    total, refs = term_sum(n_term, refs)
    coded = refs[:-1]
    for codes, exponents in zip(coded[::2], coded[1::2]):
        total = total + decoded(codes[...], exponents[...])
    refs[-1][0] = total.T if transposed else total


def finish(terms, d, extra, supers, width, transposed):
    rows, w = terms[0].shape[1:]
    share = w if transposed else rows
    tall = rows // CODE_ROWS
    if transposed:
        term = shard_specs(terms, (width, w), lambda s: (s, 0))
        codes = pl.BlockSpec((width, w), lambda s, at: (s, 0))
        exponents = pl.BlockSpec((CODE_ROWS, w), lambda s, at: (tall, 0))
    else:
        term = shard_specs(terms, (rows, width), lambda s: (0, s))
        codes = pl.BlockSpec((rows, width), lambda s, at: (0, s))
        exponents = pl.BlockSpec((CODE_ROWS, width), lambda s, at: (tall, s))
    total = pl.pallas_call(
        functools.partial(finish_kernel, len(terms), transposed),
        out_shape=jax.ShapeDtypeStruct((supers, share, width), F32),
        grid_spec=pltpu.PrefetchScalarGridSpec(
            num_scalar_prefetch=1,
            grid=(supers,),
            in_specs=term + [codes, exponents] * len(extra),
            out_specs=pl.BlockSpec((1, share, width), lambda s, at: (s, 0, 0)),
        ),
        compiler_params=params(),
        cost_estimate=cost(1000, 1000),
        name="finish",
    )(jnp.asarray(d, jnp.int32).reshape(1), *terms, *[x for x in extra for _ in range(2)])
    return jnp.transpose(total, (1, 0, 2))


def scatter_codes(terms, carried, axis, n, t):
    i = lax.axis_index(axis)
    if n == 2:
        return pick_coded(terms, [1 - i])
    return pick_coded(terms, [jnp.clip(n - 1 - t + i, 0, n - 1), jnp.clip(t - (n - 1 - i), 0, n - 1)], carried)


def scatter_move(codes, axis, n, t):
    if n == 2:
        return (swap(codes[0], axis),)
    right = lax.ppermute(codes[0], axis, [(j, j + 1) for j in range(t + 1)])
    left = lax.ppermute(codes[1], axis, [(n - 1 - j, n - 2 - j) for j in range(t + 1)])
    return (right, left)


def direct_sum(x, axis, n):
    if n & (n - 1):
        return lax.psum(x, axis)
    k = 1
    while k < n:
        x = x + lax.ppermute(x, axis, [(j, j ^ k) for j in range(n)])
        k *= 2
    return x


def halves_back(x, axis, n):
    if n != 2:
        return lax.all_gather(x, axis, axis=0, tiled=True)
    other = lax.ppermute(x, axis, [(0, 1), (1, 0)])
    swap = lax.axis_index(axis) == 1
    return jnp.concatenate([jnp.where(swap, other, x), jnp.where(swap, x, other)])


def with_unit(size, main_ref, spare_ref, buffer, sem, slot, use):
    @pl.when(jnp.logical_and(slot >= 0, slot < size.main))
    def _():
        use(main_ref[slot, 0], main_ref[slot, 1])

    if size.spare:
        with_spare(size, spare_ref, buffer, sem, slot, use)


def with_spare(size, spare_ref, buffer, sem, slot, use):
    @pl.when(slot >= size.main)
    def _():
        copy = pltpu.make_async_copy(spare_ref.at[slot - size.main], buffer, sem)
        copy.start()
        copy.wait()
        use(buffer[0], buffer[1])


def row_kernel(size, first, paired, share, source_ref, slot_ref, weight_ref, *refs):
    refs = list(refs)
    a_ref, main_ref, spare_ref = refs[:3]
    refs = refs[3:]
    n_out = 2 if paired else 1
    before = None if first else refs[:n_out]
    refs = refs[0 if first else n_out :]
    outs, (left, kept, buffer, sem) = refs[:n_out], refs[n_out:]
    units, supers, half, unit_rows = size.units, size.supers, size.width, size.unit_rows
    deep = 2 * unit_rows
    shard = source_ref[0]

    @pl.when(pl.program_id(0) == 0)
    def _():
        for s in range(supers):
            kept[s, units] = 0
            for u in range(units):
                slot = jnp.where(shard >= 0, slot_ref[(jnp.maximum(shard, 0) * units + u) * supers + s], -1)

                def build(real, imag, s=s, u=u):
                    at = kept[s, units]
                    left[s, at, :half, :unit_rows] = real
                    left[s, at, :half, unit_rows:] = -imag
                    left[s, at, half:, :unit_rows] = imag
                    left[s, at, half:, unit_rows:] = real
                    kept[s, at] = u
                    kept[s, units] = at + 1

                with_unit(size, main_ref, spare_ref, buffer, sem, slot, build)

    pole = source_ref[1]

    def store(s, mix):
        rows = pl.ds(pl.multiple_of(s * half, half), half)
        for part in range(2 if paired else 1):
            value = mix[:, part * share : (part + 1) * share] if paired else mix

            def put(out, old):
                if old is None:
                    out[0, rows, :] = -value
                else:
                    out[0, rows, :] = old[0, rows, :] - value

            if not paired:
                put(outs[0], None if first else before[0])
                continue

            @pl.when(pole == part)
            def _():
                put(outs[0], None if first else before[0])

            @pl.when(pole != part)
            def _():
                put(outs[1], None if first else before[1])

    def one(s, _):
        count = kept[s, units]

        @pl.when(count == 0)
        def _():
            store(s, jnp.zeros((half, a_ref.shape[2]), F32))

        for many in range(1, units + 1):

            @pl.when(count == many)
            def _():
                tall = []
                wide = []
                for i in range(many):
                    rows = pl.ds(pl.multiple_of(kept[s, i] * unit_rows, unit_rows), unit_rows)
                    tall += [a_ref[0, rows, :], a_ref[1, rows, :]]
                    wide.append(left[s, i])
                wide = wide[0] if many == 1 else jnp.concatenate(wide, axis=1)
                sums = jnp.dot(wide, jnp.concatenate(tall, axis=0), preferred_element_type=F32)
                store(s, weight_ref[1] * sums[:half] + weight_ref[0] * sums[half:])

        return 0

    lax.fori_loop(0, supers, one, 0)


def row_product(inverse, before, source, pole, slot, weights, pieces, size, tile, share):
    first = before is None
    part_rows, part_cols = inverse.shape[1:]
    rows = size.units * size.unit_rows
    deep = size.supers * size.width
    count = part_cols // tile
    paired = tile == 2 * share
    thin = share if paired else tile
    n_out = 2 if paired else 1
    tiles = [pl.BlockSpec((1, deep, thin), lambda j, *_: (j, 0, 0))] * n_out
    outs = [jax.ShapeDtypeStruct((count, deep, thin), F32)] * n_out
    return pl.pallas_call(
        functools.partial(row_kernel, size, first, paired, share),
        out_shape=outs,
        grid_spec=pltpu.PrefetchScalarGridSpec(
            num_scalar_prefetch=2,
            grid=(count,),
            in_specs=[smem(), pl.BlockSpec((2, rows, tile), lambda j, src, _: (0, jnp.maximum(src[0], 0), j))]
            + [whole_vmem(), any_space()]
            + ([] if first else tiles),
            out_specs=tiles,
            scratch_shapes=[
                pltpu.VMEM((size.supers, size.units, 2 * size.width, 2 * size.unit_rows), BF16),
                pltpu.SMEM((size.supers, size.units + 1), jnp.int32),
                pltpu.VMEM((2, size.width, size.unit_rows), BF16),
                pltpu.SemaphoreType.DMA,
            ],
        ),
        compiler_params=params(),
        cost_estimate=cost(1000, 1000),
        name="row_product",
    )(jnp.stack([source, pole]), slot, weights, inverse, *pieces, *([] if first else before))


def column_kernel(size, n_piece, n_source, n_upper, n_after, part_rows, n_share, first, last, source_ref, slot_ref, weight_ref, *refs):
    units, supers, width, unit_rows = size.units, size.supers, size.width, size.unit_rows
    refs = list(refs)
    acc_in = None if first else refs.pop(0)
    given_ref = refs.pop(0) if last else None
    a_ref = refs.pop(0)
    pieces = [(refs.pop(0), refs.pop(0)) for _ in range(n_piece)]
    uppers = [(refs.pop(0), refs.pop(0)) for _ in range(n_upper)]
    refs = refs[n_after:]
    if last:
        keep_out, send_out, t_ref = refs[:3]
        keep_ref, send_ref, x_sems, upper_mains, upper_buffer, upper_sems = refs[3:9]
        refs = refs[9:]
    else:
        acc_out, token_ref = refs.pop(0), refs.pop(0)
    acc, right, mains, buffer, sem, main_sems, acc_sems = refs
    step = pl.program_id(0)

    def each_load(q, act):
        for i in range(n_piece):

            @pl.when(source_ref[n_source + q] == i)
            def _():
                act(pltpu.make_async_copy(pieces[i][0], mains.at[q], main_sems.at[q]))

    acc_loads = []
    if not first:
        acc_loads = [pltpu.make_async_copy(acc_in.at[s], acc.at[s], acc_sems.at[s]) for s in range(supers)]
    acc_stores = []
    if not last:
        acc_stores = [pltpu.make_async_copy(acc.at[s], acc_out.at[s], acc_sems.at[s]) for s in range(supers)]
    upper_loads = [pltpu.make_async_copy(uppers[q][0], upper_mains.at[q], upper_sems.at[q]) for q in range(n_upper)]

    @pl.when(step == 0)
    def _():
        each_load(0, lambda load: load.start())
        for load in acc_loads:
            load.start()
        for q in range(1, n_source):
            each_load(q, lambda load: load.start())
        for load in upper_loads:
            load.start()
        if not last:
            token_ref[...] = jnp.zeros_like(token_ref)
        if first:
            acc[...] = jnp.zeros_like(acc)

    for q in range(n_source):

        @pl.when(step == q * units)
        def _():
            each_load(q, lambda load: load.wait())

    source = step // units
    place = source_ref[source] * units + step % units

    for s in range(supers):
        slot = slot_ref[place * supers + s]

        def build(real, imag):
            right[:unit_rows, :width] = real
            right[:unit_rows, width:] = imag
            right[unit_rows:, :width] = -imag
            right[unit_rows:, width:] = real

        @pl.when(jnp.logical_and(slot >= 0, slot < size.main))
        def _():
            build(mains[source, slot, 0], mains[source, slot, 1])

        if size.spare:
            for i in range(n_piece):
                here = jnp.where(source_ref[n_source + source] == i, slot, -1)
                with_spare(size, pieces[i][1], buffer, sem, here, build)

        if not first:

            @pl.when(step == 0)
            def _():
                acc_loads[s].wait()

        @pl.when(slot >= 0)
        def _():
            both = jnp.concatenate([a_ref[0], a_ref[1]], axis=1)
            acc[s] += jnp.dot(both, right[...], preferred_element_type=F32)

        if not last:

            @pl.when(step == n_source * units - 1)
            def _():
                acc_stores[s].start()

    if not last:

        @pl.when(step == n_source * units - 1)
        def _():
            for store in acc_stores:
                store.wait()

        return

    @pl.when(step == n_source * units - 1)
    def _():
        weight_real = weight_ref[0]
        weight_imag = weight_ref[1]
        pole = source_ref[2 * n_source + n_upper]
        share = part_rows // n_share
        for load in upper_loads:
            load.wait()
        for k in range(n_share):
            rows = slice(k * share, (k + 1) * share)
            for part, out in ((0, keep_ref), (1, send_ref)):

                @pl.when((pole == k % 2) == (part == 0))
                def _():
                    for s in range(supers):
                        out[k // 2, :, s * width : (s + 1) * width] = -(
                            weight_imag * acc[s, rows, :width] + weight_real * acc[s, rows, width:]
                        )

        x_stores = [
            pltpu.make_async_copy(keep_ref, keep_out, x_sems.at[0]),
            pltpu.make_async_copy(send_ref, send_out, x_sems.at[1]),
        ]
        for store in x_stores:
            store.start()

        t_ref[...] = given_ref[...]

        def unit(k, _):
            rows = pl.ds(pl.multiple_of(k * unit_rows, unit_rows), unit_rows)
            upper = jnp.int32(0)
            for q in range(n_upper):
                upper = jnp.where(source_ref[2 * n_source + q] == k // units, q, upper)
            for s in range(supers):
                slot = slot_ref[n_slots + k * supers + s]

                def use(real, imag):
                    first_acc = acc[s, rows, :width]
                    second_acc = acc[s, rows, width:]
                    mix = weight_imag * first_acc + weight_real * second_acc
                    other = weight_real * first_acc - weight_imag * second_acc
                    stacked = jnp.concatenate([mix, other], axis=0)
                    high = stacked.astype(BF16)
                    low = (stacked - high.astype(F32)).astype(BF16)
                    both = jnp.concatenate([real, imag], axis=1)
                    sums = jnp.dot(both, jnp.concatenate([high, low], axis=1), preferred_element_type=F32)
                    t_ref[s] += sums[:, :width] + sums[:, width:]

                @pl.when(jnp.logical_and(slot >= 0, slot < size.main))
                def _():
                    use(upper_mains[upper, slot, 0], upper_mains[upper, slot, 1])

                if size.spare:
                    for q in range(n_upper):
                        with_spare(size, uppers[q][1], upper_buffer, sem, jnp.where(upper == q, slot, -1), use)

            return 0

        n_slots = slot_ref.shape[0] - part_rows // unit_rows * supers
        lax.fori_loop(0, part_rows // unit_rows, unit, 0)
        for store in x_stores:
            store.wait()


def column_phase(inverse, acc, sources, which, positions, slot, weights, pieces, uppers, size, n_col, given=(), after=()):
    first, last = acc is None, bool(uppers)
    n_source, n_upper = len(sources), len(uppers)
    part_rows, part_cols = inverse.shape[1:]
    units, unit_rows, supers, width = size.units, size.unit_rows, size.supers, size.width
    flat = [p for group in pieces + uppers for p in group]

    prefetch = jnp.stack(list(sources) + list(which) + list(positions)).astype(jnp.int32)

    def a_map(g, src, _):
        return (0, 0, src[g // units] * units + g % units)

    acc_shape = (supers, part_rows, 2 * width)
    in_specs = [smem()] + ([] if first else [any_space()]) + ([whole_vmem()] if last else [])
    in_specs += [pl.BlockSpec((2, part_rows, unit_rows), a_map)] + [any_space()] * (len(flat) + len(after))
    scratch = [
        pltpu.VMEM((2 * unit_rows, 2 * width), BF16),
        pltpu.VMEM((n_source, size.main, 2, unit_rows, width), BF16),
        pltpu.VMEM((2, unit_rows, width), BF16),
        pltpu.SemaphoreType.DMA,
        pltpu.SemaphoreType.DMA((n_source,)),
        pltpu.SemaphoreType.DMA((supers,)),
    ]
    scratch.insert(0, pltpu.VMEM(acc_shape, F32))
    if last:
        out_shape = [jax.ShapeDtypeStruct((n_col, part_rows // (2 * n_col), supers * width), F32)] * 2
        out_shape.append(jax.ShapeDtypeStruct((supers, width, width), F32))
        scratch = [
            pltpu.VMEM(out_shape[0].shape, F32),
            pltpu.VMEM(out_shape[0].shape, F32),
            pltpu.SemaphoreType.DMA((2,)),
            pltpu.VMEM((n_upper, size.main, 2, width, unit_rows), BF16),
            pltpu.VMEM((2, width, unit_rows), BF16),
            pltpu.SemaphoreType.DMA((n_upper,)),
        ] + scratch
        out_specs = [any_space(), any_space(), whole_vmem()]
    else:
        out_shape = [jax.ShapeDtypeStruct(acc_shape, F32), jax.ShapeDtypeStruct((8, 128), F32)]
        out_specs = [any_space(), whole_vmem()]
    return pl.pallas_call(
        functools.partial(
            column_kernel, size, len(pieces), n_source, n_upper, len(after), part_rows, 2 * n_col, first, last
        ),
        out_shape=out_shape,
        grid_spec=pltpu.PrefetchScalarGridSpec(
            num_scalar_prefetch=2,
            grid=(n_source * units,),
            in_specs=in_specs,
            out_specs=out_specs,
            scratch_shapes=scratch,
        ),
        compiler_params=params(),
        cost_estimate=cost(1000, 1000),
        name="column_phase",
    )(prefetch, slot, weights, *([] if first else [acc]), *given, inverse, *flat, *after)


def body(inverse, lower, upper, diag_inverse, weights, pattern):
    n_row = lax.axis_size("row")
    n_col = lax.axis_size("col")
    n_pole = lax.axis_size("pole")
    assert n_pole == 2
    row_index = lax.axis_index("row")
    col_index = lax.axis_index("col")
    pole_index = lax.axis_index("pole")
    local_rows, _, supers, width = lower.shape[1:]
    inverse = inverse[0]
    part_rows, part_cols = inverse.shape[1:]
    unit_rows = min(width, local_rows)
    units = local_rows // unit_rows
    size = Sizes(units, supers, unit_rows, width)
    weight = weights[0]
    lower_from = [(row_index,)] + hop_sources(row_index, n_row)
    upper_from = [p for pair in hop_sources(col_index, n_col) for p in pair]

    slot, most = unit_tables(pattern, n_row * n_col, units, unit_rows, width)
    crowded = most > size.main
    row_slot = lax.dynamic_slice_in_dim(slot, row_index * n_col, n_col, 0).reshape(-1)
    col_slot = lax.dynamic_slice_in_dim(slot, col_index * n_row, n_row, 0).reshape(-1)
    lower_parts = jnp.transpose(lower[0], (1, 2, 0, 3))
    own_lower, spare_lower = pack(lower_parts, pick(slot, col_index * n_row + row_index), size, False)
    own_lower, spare_lower, upper = fence((own_lower, spare_lower, upper))
    upper_parts = jnp.transpose(upper[0], (1, 2, 0, 3))
    own_upper = pack(upper_parts, pick(slot, row_index * n_col + col_index), size, True)

    def first_part(size):
        def run(own_upper, own_lower, spare_lower):
            sums = row_product(inverse, None, col_index, pole_index, row_slot, weight, own_upper, size, tile, share)
            sums, own_lower = fence((sums, own_lower))
            pieces = [(own_lower, spare_lower)]
            acc, token = column_phase(
                inverse, None, [row_index], [jnp.int32(0)], [], col_slot, weight, pieces, [], size, n_col
            )
            return sums, acc, token

        return run

    given = diag_inverse[0].astype(F32)
    own_term = weight[0] * given[:, 1] + weight[1] * given[:, 0]
    owner = jnp.logical_and(row_index == 0, col_index == 0)
    own_term = jnp.where(owner, own_term, 0.0)

    tile = min(1024, part_cols)
    share = part_cols // (n_row * n_pole)
    passing = hop((own_lower,), "row", n_row, 1)
    upper_got = [p for pair in line_gather(own_upper[0], "col", n_col) for p in pair]
    sums, acc, token = lax.cond(
        crowded, first_part(size), first_part(size.usual()), own_upper, own_lower, spare_lower
    )
    passing, own_upper, upper_got, sums, token, own_term = fence(
        (passing, own_upper, upper_got, sums, token, own_term)
    )

    def send(pieces):
        return jax.tree.leaves([line_gather(pieces[0], "row", n_row), line_gather(pieces[1], "col", n_col)])

    def skip(pieces):
        return list(blank(jax.eval_shape(send, pieces)))

    spread = lax.cond(crowded, send, skip, (spare_lower, own_upper[1]))
    row_spares, col_spares = spread[: len(spread) - len(upper_got)], spread[len(spread) - len(upper_got) :]
    uppers = [own_upper] + list(zip(upper_got, col_spares))

    def second_part(size):
        def run(sums, got, col_spares):
            for source, *pieces in zip(upper_from, got, col_spares):
                sums = row_product(inverse, sums, source, pole_index, row_slot, weight, pieces, size, tile, share)
            if len(sums) == 2:
                terms = (sums[0], swap(sums[1], "pole"))
            else:
                both = jnp.transpose(sums[0], (1, 0, 2)).reshape(supers * width, n_row, n_pole, share)
                both = jnp.transpose(both, (2, 1, 0, 3))
                terms = (pick(both, pole_index), swap(pick(both, 1 - pole_index), "pole"))
            return terms, scatter_codes(terms, (), "row", n_row, 0)

        return run

    held = [(1, passing)]
    if n_row > 2:
        passing = hop(passing, "row", n_row, 2)
    terms, codes = lax.cond(
        crowded, second_part(size), second_part(size.usual()), sums, upper_got, col_spares
    )
    passing, terms, codes = fence((passing, terms, codes))

    def spare_pair(t):
        return row_spares[(t - 1) * len(held[-1][1]) : t * len(held[-1][1])]

    brought = [p for hop_pair in lower_from[1:] for p in hop_pair]
    rank = [jnp.int32(0)]
    for p in brought:
        rank.append(rank[-1] + (p >= 0))

    def nth(j, values):
        found = jnp.int32(0)
        for i, p in enumerate(brought):
            found = jnp.where(jnp.logical_and(p >= 0, rank[i] == j), values[i], found)
        return found

    def phase(acc, held, last):
        pieces = [p for t, pair in held for p in zip(pair, spare_pair(t))]
        taken = [n_row - 2] if last else range(n_row - 2)
        sources = [nth(j, brought) for j in taken]
        which = [nth(j, range(len(brought))) for j in taken]
        if not last:
            return column_phase(inverse, acc, sources, which, [], col_slot, weight, pieces, [], size, n_col)
        positions = [col_index] + upper_from + [pole_index]
        slots = jnp.concatenate([col_slot, row_slot])
        return column_phase(
            inverse, acc, sources, which, positions, slots, weight, pieces, uppers, size, n_col, (own_term,), (token,)
        )

    stage = 0
    carried = ()
    for t in range(3, n_row):
        held.append((t - 1, passing))
        passing = hop(passing, "row", n_row, t)
        carried = scatter_move(codes, "row", n_row, stage)
        stage += 1
        if t == n_row - 1:
            acc, token = phase(acc, held, False)
        codes = scatter_codes(terms, carried, "row", n_row, stage)
        passing, token, terms, codes = fence((passing, token, terms, codes))
    if n_row > 2:
        held.append((n_row - 1, passing))
        carried = scatter_move(codes, "row", n_row, stage)
        stage += 1
    keep, give, t_part = phase(acc, held, True)
    keep, give, t_part, terms, carried, codes = fence((keep, give, t_part, terms, carried, codes))
    if n_row > 2:
        codes = scatter_codes(terms, carried, "row", n_row, stage)

    carried = scatter_move(codes, "row", n_row, stage)
    col_terms = (keep, swap(give, "pole"))
    col_codes = scatter_codes(col_terms, (), "col", n_col, 0)

    t_part = t_part.reshape(n_pole, -1, width)
    t_sum = pick(t_part, pole_index) + swap(pick(t_part, 1 - pole_index), "pole")
    if n_col == 2:
        t_sum = t_sum.reshape(n_col, -1, width)
        t_sum = pick(t_sum, col_index) + swap(pick(t_sum, 1 - col_index), "col")
    else:
        t_sum = direct_sum(t_sum, "col", n_col)
    t_sum, col_codes, carried = fence((t_sum, col_codes, carried))
    for t in range(n_col - 1):
        col_carried = scatter_move(col_codes, "col", n_col, t)
        if t < n_col - 2:
            col_codes = scatter_codes(col_terms, col_carried, "col", n_col, t + 1)
    t_sum = direct_sum(t_sum, "row", n_row)
    row_density = finish(terms, row_index, carried, supers, width, True)
    t_sum, col_carried, row_density = fence((t_sum, col_carried, row_density))
    column_density = finish(col_terms, col_index, col_carried, supers, width, False)
    if n_col == 2:
        t_sum = halves_back(t_sum, "col", n_col)
    t_sum, column_density = fence((t_sum, column_density))
    diagonal_density = halves_back(t_sum, "pole", n_pole).reshape(supers, width, width)
    return (column_density, row_density, diagonal_density)


def solution(mesh):
    return jax.shard_map(
        body,
        mesh=mesh,
        in_specs=(
            P(("groups", "pole"), None, "row", "col"),
            P(("groups", "pole"), ("col", "row"), None, None, None),
            P(("groups", "pole"), ("row", "col"), None, None, None),
            P(("groups", "pole"), None, None, None, None),
            P(("groups", "pole"), None),
            P("groups", None),
        ),
        out_specs=(
            P(("groups", "row", "col", "pole"), None, None),
            P(("groups", "col", "row", "pole"), None, None),
            P("groups", None, None),
        ),
        check_vma=False,
    )
```

```python
import functools

import jax
import jax.numpy as jnp
from jax import lax
from jax.experimental import pallas as pl
from jax.experimental.pallas import tpu as pltpu
from jax.sharding import PartitionSpec as P

VMEM_LIMIT = 46 * 1024 * 1024
F32 = jnp.float32
BF16 = jnp.bfloat16


def params(limit=VMEM_LIMIT, **kw):
    return pltpu.CompilerParams(vmem_limit_bytes=limit, **kw)


def cost(flops, nbytes):
    return pl.CostEstimate(flops=int(flops), bytes_accessed=int(nbytes), transcendentals=0)


def fence(tree):
    return lax.optimization_barrier(tree)


def whole_vmem():
    return pl.BlockSpec(memory_space=pltpu.VMEM)


def smem():
    return pl.BlockSpec(memory_space=pltpu.SMEM)


def unit_tables(pattern, shards, units, unit_rows, width):
    supers = pattern.shape[0]
    block = (lax.iota(jnp.int32, shards * units) * unit_rows) // width
    hits = jnp.any(pattern[:, :, None] == block[None, None, :], axis=1)
    flags = jnp.transpose(hits).reshape(shards, units * supers).astype(jnp.int32)
    places = lax.iota(jnp.int32, units * supers)
    before = (places[:, None] < places[None, :]).astype(jnp.int32)
    rank = jnp.sum(flags[:, :, None] * before[None], axis=1)
    slot = jnp.where(flags > 0, rank, -1)
    most = jnp.max(jnp.sum(flags, axis=1))
    return slot, most


class Sizes:
    def __init__(self, units, supers, unit_rows, width):
        self.units, self.supers, self.unit_rows, self.width = units, supers, unit_rows, width
        self.main = units * max(supers - 1, 1)
        self.spare = units * supers - self.main

    def usual(self):
        size = Sizes(self.units, self.supers, self.unit_rows, self.width)
        size.spare = 0
        return size


def any_space():
    return pl.BlockSpec(memory_space=pl.ANY)


def pack_kernel(size, transposed, slot_ref, x_ref, main_ref, spare_ref):
    rows = size.unit_rows
    for u in range(size.units):
        for s in range(size.supers):
            slot = slot_ref[u * size.supers + s]

            def store(ref, at):
                for h in range(2):
                    tile = x_ref[h, s, u * rows : (u + 1) * rows, :]
                    ref[at, h] = tile.T if transposed else tile

            @pl.when(jnp.logical_and(slot >= 0, slot < size.main))
            def _():
                store(main_ref, slot)

            if size.spare:

                @pl.when(slot >= size.main)
                def _():
                    store(spare_ref, slot - size.main)


def pack(x, slot, size, transposed):
    tile = (2, size.width, size.unit_rows) if transposed else (2, size.unit_rows, size.width)
    return pl.pallas_call(
        functools.partial(pack_kernel, size, transposed),
        out_shape=[
            jax.ShapeDtypeStruct((size.main,) + tile, x.dtype),
            jax.ShapeDtypeStruct((max(size.units * size.supers - size.main, 1),) + tile, x.dtype),
        ],
        in_specs=[smem(), whole_vmem()],
        out_specs=[whole_vmem()] * 2,
        compiler_params=params(),
        cost_estimate=cost(1000, 1000),
        name="pack",
    )(slot, x)


def blank(like):
    return pl.pallas_call(
        lambda *refs: None,
        out_shape=tuple(like),
        out_specs=[any_space()] * len(like),
        compiler_params=params(has_side_effects=True),
        name="blank",
    )()


def swap(x, axis):
    return lax.ppermute(x, axis, [(0, 1), (1, 0)])


def hop(pair, axis, n, t):
    if n == 2:
        return (swap(pair[0], axis),)
    right = lax.ppermute(pair[0], axis, [(i, i + 1) for i in range(t - 1, n - 1)])
    left = lax.ppermute(pair[-1], axis, [(i + 1, i) for i in range(0, n - t)])
    return (right, left)


def line_gather(x, axis, n):
    hops = [(x,)]
    for t in range(1, n):
        hops.append(hop(hops[-1], axis, n, t))
    return hops[1:]


def hop_sources(index, n):
    if n == 2:
        return [(1 - index,)]
    return [
        (jnp.where(index - t >= 0, index - t, -1), jnp.where(index + t < n, index + t, -1)) for t in range(1, n)
    ]


def pick(shards, d):
    return lax.dynamic_index_in_dim(shards, d, 0, keepdims=False)


CODE_ROWS = 16


def decoded(codes, exponents):
    return codes.astype(jnp.int32).astype(F32) * jnp.exp2(exponents[:1].astype(jnp.int32).astype(F32))


def shard_specs(terms, shape, place):
    return [pl.BlockSpec((1,) + shape, lambda j, at: (at[0],) + place(j))] * len(terms)


def term_sum(n_term, refs):
    return functools.reduce(jnp.add, [ref[0] for ref in refs[:n_term]]), refs[n_term:]


def encode(total, out):
    rows = total.shape[0]
    most = jnp.maximum(jnp.max(jnp.abs(total), axis=0, keepdims=True), 1e-30)
    exponent = jnp.ceil(jnp.log2(most) + 0.01) - 15.0
    codes = jnp.floor(total * jnp.exp2(-exponent) + 0.5)
    out[:rows, :] = codes.astype(jnp.int32).astype(jnp.int16)
    out[rows:, :] = jnp.broadcast_to(exponent, (CODE_ROWS, exponent.shape[1])).astype(jnp.int32).astype(jnp.int16)


def pick_kernel(n_term, n_way, rows, index_ref, *refs):
    terms, extras, outs = refs[:n_term], refs[n_term:-n_way], refs[-n_way:]
    for way in range(n_way):

        @pl.when(pl.program_id(0) == way)
        def _():
            mine = functools.reduce(jnp.add, [ref[0] for ref in terms])
            if extras:
                mine = mine + decoded(extras[way][:rows, :], extras[way][rows:, :])
            encode(mine, outs[way])


def pick_coded(terms, shards, extra=()):
    rows, w = terms[0].shape[1:]
    step = next((k for k in (512, 256) if w % k == 0), w)
    steps = w // step
    n_way = len(shards)

    def coded(way):
        def place(g, j, at):
            return (0, jnp.where(g == way, j, jnp.where(g < way, 0, steps - 1)))

        return pl.BlockSpec((rows + CODE_ROWS, step), place)

    ways = [coded(way) for way in range(n_way)]
    return pl.pallas_call(
        functools.partial(pick_kernel, len(terms), n_way, rows),
        out_shape=[jax.ShapeDtypeStruct((rows + CODE_ROWS, w), jnp.int16)] * n_way,
        grid_spec=pltpu.PrefetchScalarGridSpec(
            num_scalar_prefetch=1,
            grid=(n_way, steps),
            in_specs=[pl.BlockSpec((1, rows, step), lambda g, j, at: (at[g], 0, j))] * len(terms)
            + (ways if extra else []),
            out_specs=ways,
        ),
        compiler_params=params(),
        cost_estimate=cost(1000, 1000),
        name="pick_coded",
    )(jnp.stack(shards).astype(jnp.int32), *terms, *extra)


def finish_kernel(n_term, transposed, index_ref, *refs):
    total, refs = term_sum(n_term, refs)
    coded = refs[:-1]
    for codes, exponents in zip(coded[::2], coded[1::2]):
        total = total + decoded(codes[...], exponents[...])
    refs[-1][0] = total.T if transposed else total


def finish(terms, d, extra, supers, width, transposed):
    rows, w = terms[0].shape[1:]
    share = w if transposed else rows
    tall = rows // CODE_ROWS
    if transposed:
        term = shard_specs(terms, (width, w), lambda s: (s, 0))
        codes = pl.BlockSpec((width, w), lambda s, at: (s, 0))
        exponents = pl.BlockSpec((CODE_ROWS, w), lambda s, at: (tall, 0))
    else:
        term = shard_specs(terms, (rows, width), lambda s: (0, s))
        codes = pl.BlockSpec((rows, width), lambda s, at: (0, s))
        exponents = pl.BlockSpec((CODE_ROWS, width), lambda s, at: (tall, s))
    total = pl.pallas_call(
        functools.partial(finish_kernel, len(terms), transposed),
        out_shape=jax.ShapeDtypeStruct((supers, share, width), F32),
        grid_spec=pltpu.PrefetchScalarGridSpec(
            num_scalar_prefetch=1,
            grid=(supers,),
            in_specs=term + [codes, exponents] * len(extra),
            out_specs=pl.BlockSpec((1, share, width), lambda s, at: (s, 0, 0)),
        ),
        compiler_params=params(),
        cost_estimate=cost(1000, 1000),
        name="finish",
    )(jnp.asarray(d, jnp.int32).reshape(1), *terms, *[x for x in extra for _ in range(2)])
    return jnp.transpose(total, (1, 0, 2))


def scatter_codes(terms, carried, axis, n, t):
    i = lax.axis_index(axis)
    if n == 2:
        return pick_coded(terms, [1 - i])
    return pick_coded(terms, [jnp.clip(n - 1 - t + i, 0, n - 1), jnp.clip(t - (n - 1 - i), 0, n - 1)], carried)


def scatter_move(codes, axis, n, t):
    if n == 2:
        return (swap(codes[0], axis),)
    right = lax.ppermute(codes[0], axis, [(j, j + 1) for j in range(t + 1)])
    left = lax.ppermute(codes[1], axis, [(n - 1 - j, n - 2 - j) for j in range(t + 1)])
    return (right, left)


def direct_sum(x, axis, n):
    if n & (n - 1):
        return lax.psum(x, axis)
    k = 1
    while k < n:
        x = x + lax.ppermute(x, axis, [(j, j ^ k) for j in range(n)])
        k *= 2
    return x


def halves_back(x, axis, n):
    if n != 2:
        return lax.all_gather(x, axis, axis=0, tiled=True)
    other = lax.ppermute(x, axis, [(0, 1), (1, 0)])
    swap = lax.axis_index(axis) == 1
    return jnp.concatenate([jnp.where(swap, other, x), jnp.where(swap, x, other)])


def with_unit(size, main_ref, spare_ref, buffer, sem, slot, use):
    @pl.when(jnp.logical_and(slot >= 0, slot < size.main))
    def _():
        use(main_ref[slot, 0], main_ref[slot, 1])

    if size.spare:
        with_spare(size, spare_ref, buffer, sem, slot, use)


def with_spare(size, spare_ref, buffer, sem, slot, use):
    @pl.when(slot >= size.main)
    def _():
        copy = pltpu.make_async_copy(spare_ref.at[slot - size.main], buffer, sem)
        copy.start()
        copy.wait()
        use(buffer[0], buffer[1])


def row_kernel(size, first, paired, share, source_ref, slot_ref, weight_ref, *refs):
    refs = list(refs)
    a_ref, main_ref, spare_ref = refs[:3]
    refs = refs[3:]
    n_out = 2 if paired else 1
    before = None if first else refs[:n_out]
    refs = refs[0 if first else n_out :]
    outs, (left, kept, buffer, sem) = refs[:n_out], refs[n_out:]
    units, supers, half, unit_rows = size.units, size.supers, size.width, size.unit_rows
    deep = 2 * unit_rows
    shard = source_ref[0]

    @pl.when(pl.program_id(0) == 0)
    def _():
        for s in range(supers):
            kept[s, units] = 0
            for u in range(units):
                slot = jnp.where(shard >= 0, slot_ref[(jnp.maximum(shard, 0) * units + u) * supers + s], -1)

                def build(real, imag, s=s, u=u):
                    at = kept[s, units]
                    left[s, at, :half, :unit_rows] = real
                    left[s, at, :half, unit_rows:] = -imag
                    left[s, at, half:, :unit_rows] = imag
                    left[s, at, half:, unit_rows:] = real
                    kept[s, at] = u
                    kept[s, units] = at + 1

                with_unit(size, main_ref, spare_ref, buffer, sem, slot, build)

    pole = source_ref[1]

    def store(s, mix):
        rows = pl.ds(pl.multiple_of(s * half, half), half)
        for part in range(2 if paired else 1):
            value = mix[:, part * share : (part + 1) * share] if paired else mix

            def put(out, old):
                if old is None:
                    out[0, rows, :] = -value
                else:
                    out[0, rows, :] = old[0, rows, :] - value

            if not paired:
                put(outs[0], None if first else before[0])
                continue

            @pl.when(pole == part)
            def _():
                put(outs[0], None if first else before[0])

            @pl.when(pole != part)
            def _():
                put(outs[1], None if first else before[1])

    def one(s, _):
        count = kept[s, units]

        @pl.when(count == 0)
        def _():
            store(s, jnp.zeros((half, a_ref.shape[2]), F32))

        for many in range(1, units + 1):

            @pl.when(count == many)
            def _():
                tall = []
                wide = []
                for i in range(many):
                    rows = pl.ds(pl.multiple_of(kept[s, i] * unit_rows, unit_rows), unit_rows)
                    tall += [a_ref[0, rows, :], a_ref[1, rows, :]]
                    wide.append(left[s, i])
                wide = wide[0] if many == 1 else jnp.concatenate(wide, axis=1)
                sums = jnp.dot(wide, jnp.concatenate(tall, axis=0), preferred_element_type=F32)
                store(s, weight_ref[1] * sums[:half] + weight_ref[0] * sums[half:])

        return 0

    lax.fori_loop(0, supers, one, 0)


def row_product(inverse, before, source, pole, slot, weights, pieces, size, tile, share):
    first = before is None
    part_rows, part_cols = inverse.shape[1:]
    rows = size.units * size.unit_rows
    deep = size.supers * size.width
    count = part_cols // tile
    paired = tile == 2 * share
    thin = share if paired else tile
    n_out = 2 if paired else 1
    tiles = [pl.BlockSpec((1, deep, thin), lambda j, *_: (j, 0, 0))] * n_out
    outs = [jax.ShapeDtypeStruct((count, deep, thin), F32)] * n_out
    return pl.pallas_call(
        functools.partial(row_kernel, size, first, paired, share),
        out_shape=outs,
        grid_spec=pltpu.PrefetchScalarGridSpec(
            num_scalar_prefetch=2,
            grid=(count,),
            in_specs=[smem(), pl.BlockSpec((2, rows, tile), lambda j, src, _: (0, jnp.maximum(src[0], 0), j))]
            + [whole_vmem(), any_space()]
            + ([] if first else tiles),
            out_specs=tiles,
            scratch_shapes=[
                pltpu.VMEM((size.supers, size.units, 2 * size.width, 2 * size.unit_rows), BF16),
                pltpu.SMEM((size.supers, size.units + 1), jnp.int32),
                pltpu.VMEM((2, size.width, size.unit_rows), BF16),
                pltpu.SemaphoreType.DMA,
            ],
        ),
        compiler_params=params(),
        cost_estimate=cost(1000, 1000),
        name="row_product",
    )(jnp.stack([source, pole]), slot, weights, inverse, *pieces, *([] if first else before))


def column_kernel(size, n_piece, n_source, n_upper, n_after, part_rows, n_share, first, last, source_ref, slot_ref, weight_ref, *refs):
    units, supers, width, unit_rows = size.units, size.supers, size.width, size.unit_rows
    refs = list(refs)
    acc_in = None if first else refs.pop(0)
    given_ref = refs.pop(0) if last else None
    a_ref = refs.pop(0)
    pieces = [(refs.pop(0), refs.pop(0)) for _ in range(n_piece)]
    uppers = [(refs.pop(0), refs.pop(0)) for _ in range(n_upper)]
    refs = refs[n_after:]
    if last:
        keep_out, send_out, t_ref = refs[:3]
        keep_ref, send_ref, x_sems, upper_mains, upper_buffer, upper_sems = refs[3:9]
        refs = refs[9:]
    else:
        acc_out, token_ref = refs.pop(0), refs.pop(0)
    acc, right, mains, buffer, sem, main_sems, acc_sems = refs
    step = pl.program_id(0)

    def each_load(q, act):
        for i in range(n_piece):

            @pl.when(source_ref[n_source + q] == i)
            def _():
                act(pltpu.make_async_copy(pieces[i][0], mains.at[q], main_sems.at[q]))

    acc_loads = []
    if not first:
        acc_loads = [pltpu.make_async_copy(acc_in.at[s], acc.at[s], acc_sems.at[s]) for s in range(supers)]
    acc_stores = []
    if not last:
        acc_stores = [pltpu.make_async_copy(acc.at[s], acc_out.at[s], acc_sems.at[s]) for s in range(supers)]
    upper_loads = [pltpu.make_async_copy(uppers[q][0], upper_mains.at[q], upper_sems.at[q]) for q in range(n_upper)]

    @pl.when(step == 0)
    def _():
        each_load(0, lambda load: load.start())
        for load in acc_loads:
            load.start()
        for q in range(1, n_source):
            each_load(q, lambda load: load.start())
        for load in upper_loads:
            load.start()
        if not last:
            token_ref[...] = jnp.zeros_like(token_ref)
        if first:
            acc[...] = jnp.zeros_like(acc)

    for q in range(n_source):

        @pl.when(step == q * units)
        def _():
            each_load(q, lambda load: load.wait())

    source = step // units
    place = source_ref[source] * units + step % units

    for s in range(supers):
        slot = slot_ref[place * supers + s]

        def build(real, imag):
            right[:unit_rows, :width] = real
            right[:unit_rows, width:] = imag
            right[unit_rows:, :width] = -imag
            right[unit_rows:, width:] = real

        @pl.when(jnp.logical_and(slot >= 0, slot < size.main))
        def _():
            build(mains[source, slot, 0], mains[source, slot, 1])

        if size.spare:
            for i in range(n_piece):
                here = jnp.where(source_ref[n_source + source] == i, slot, -1)
                with_spare(size, pieces[i][1], buffer, sem, here, build)

        if not first:

            @pl.when(step == 0)
            def _():
                acc_loads[s].wait()

        @pl.when(slot >= 0)
        def _():
            both = jnp.concatenate([a_ref[0], a_ref[1]], axis=1)
            acc[s] += jnp.dot(both, right[...], preferred_element_type=F32)

        if not last:

            @pl.when(step == n_source * units - 1)
            def _():
                acc_stores[s].start()

    if not last:

        @pl.when(step == n_source * units - 1)
        def _():
            for store in acc_stores:
                store.wait()

        return

    @pl.when(step == n_source * units - 1)
    def _():
        weight_real = weight_ref[0]
        weight_imag = weight_ref[1]
        pole = source_ref[2 * n_source + n_upper]
        share = part_rows // n_share
        for load in upper_loads:
            load.wait()
        for k in range(n_share):
            rows = slice(k * share, (k + 1) * share)
            for part, out in ((0, keep_ref), (1, send_ref)):

                @pl.when((pole == k % 2) == (part == 0))
                def _():
                    for s in range(supers):
                        out[k // 2, :, s * width : (s + 1) * width] = -(
                            weight_imag * acc[s, rows, :width] + weight_real * acc[s, rows, width:]
                        )

        x_stores = [
            pltpu.make_async_copy(keep_ref, keep_out, x_sems.at[0]),
            pltpu.make_async_copy(send_ref, send_out, x_sems.at[1]),
        ]
        for store in x_stores:
            store.start()

        t_ref[...] = given_ref[...]

        def unit(k, _):
            rows = pl.ds(pl.multiple_of(k * unit_rows, unit_rows), unit_rows)
            upper = jnp.int32(0)
            for q in range(n_upper):
                upper = jnp.where(source_ref[2 * n_source + q] == k // units, q, upper)
            for s in range(supers):
                slot = slot_ref[n_slots + k * supers + s]

                def use(real, imag):
                    first_acc = acc[s, rows, :width]
                    second_acc = acc[s, rows, width:]
                    mix = weight_imag * first_acc + weight_real * second_acc
                    other = weight_real * first_acc - weight_imag * second_acc
                    stacked = jnp.concatenate([mix, other], axis=0)
                    high = stacked.astype(BF16)
                    low = (stacked - high.astype(F32)).astype(BF16)
                    both = jnp.concatenate([real, imag], axis=1)
                    sums = jnp.dot(both, jnp.concatenate([high, low], axis=1), preferred_element_type=F32)
                    t_ref[s] += sums[:, :width] + sums[:, width:]

                @pl.when(jnp.logical_and(slot >= 0, slot < size.main))
                def _():
                    use(upper_mains[upper, slot, 0], upper_mains[upper, slot, 1])

                if size.spare:
                    for q in range(n_upper):
                        with_spare(size, uppers[q][1], upper_buffer, sem, jnp.where(upper == q, slot, -1), use)

            return 0

        n_slots = slot_ref.shape[0] - part_rows // unit_rows * supers
        lax.fori_loop(0, part_rows // unit_rows, unit, 0)
        for store in x_stores:
            store.wait()


def column_phase(inverse, acc, sources, which, positions, slot, weights, pieces, uppers, size, n_col, given=(), after=()):
    first, last = acc is None, bool(uppers)
    n_source, n_upper = len(sources), len(uppers)
    part_rows, part_cols = inverse.shape[1:]
    units, unit_rows, supers, width = size.units, size.unit_rows, size.supers, size.width
    flat = [p for group in pieces + uppers for p in group]

    prefetch = jnp.stack(list(sources) + list(which) + list(positions)).astype(jnp.int32)

    def a_map(g, src, _):
        return (0, 0, src[g // units] * units + g % units)

    acc_shape = (supers, part_rows, 2 * width)
    in_specs = [smem()] + ([] if first else [any_space()]) + ([whole_vmem()] if last else [])
    in_specs += [pl.BlockSpec((2, part_rows, unit_rows), a_map)] + [any_space()] * (len(flat) + len(after))
    scratch = [
        pltpu.VMEM((2 * unit_rows, 2 * width), BF16),
        pltpu.VMEM((n_source, size.main, 2, unit_rows, width), BF16),
        pltpu.VMEM((2, unit_rows, width), BF16),
        pltpu.SemaphoreType.DMA,
        pltpu.SemaphoreType.DMA((n_source,)),
        pltpu.SemaphoreType.DMA((supers,)),
    ]
    scratch.insert(0, pltpu.VMEM(acc_shape, F32))
    if last:
        out_shape = [jax.ShapeDtypeStruct((n_col, part_rows // (2 * n_col), supers * width), F32)] * 2
        out_shape.append(jax.ShapeDtypeStruct((supers, width, width), F32))
        scratch = [
            pltpu.VMEM(out_shape[0].shape, F32),
            pltpu.VMEM(out_shape[0].shape, F32),
            pltpu.SemaphoreType.DMA((2,)),
            pltpu.VMEM((n_upper, size.main, 2, width, unit_rows), BF16),
            pltpu.VMEM((2, width, unit_rows), BF16),
            pltpu.SemaphoreType.DMA((n_upper,)),
        ] + scratch
        out_specs = [any_space(), any_space(), whole_vmem()]
    else:
        out_shape = [jax.ShapeDtypeStruct(acc_shape, F32), jax.ShapeDtypeStruct((8, 128), F32)]
        out_specs = [any_space(), whole_vmem()]
    return pl.pallas_call(
        functools.partial(
            column_kernel, size, len(pieces), n_source, n_upper, len(after), part_rows, 2 * n_col, first, last
        ),
        out_shape=out_shape,
        grid_spec=pltpu.PrefetchScalarGridSpec(
            num_scalar_prefetch=2,
            grid=(n_source * units,),
            in_specs=in_specs,
            out_specs=out_specs,
            scratch_shapes=scratch,
        ),
        compiler_params=params(),
        cost_estimate=cost(1000, 1000),
        name="column_phase",
    )(prefetch, slot, weights, *([] if first else [acc]), *given, inverse, *flat, *after)


def body(inverse, lower, upper, diag_inverse, weights, pattern):
    n_row = lax.axis_size("row")
    n_col = lax.axis_size("col")
    n_pole = lax.axis_size("pole")
    assert n_pole == 2
    row_index = lax.axis_index("row")
    col_index = lax.axis_index("col")
    pole_index = lax.axis_index("pole")
    local_rows, _, supers, width = lower.shape[1:]
    inverse = inverse[0]
    part_rows, part_cols = inverse.shape[1:]
    unit_rows = min(width, local_rows)
    units = local_rows // unit_rows
    size = Sizes(units, supers, unit_rows, width)
    weight = weights[0]
    lower_from = [(row_index,)] + hop_sources(row_index, n_row)
    upper_from = [p for pair in hop_sources(col_index, n_col) for p in pair]

    slot, most = unit_tables(pattern, n_row * n_col, units, unit_rows, width)
    crowded = most > size.main
    row_slot = lax.dynamic_slice_in_dim(slot, row_index * n_col, n_col, 0).reshape(-1)
    col_slot = lax.dynamic_slice_in_dim(slot, col_index * n_row, n_row, 0).reshape(-1)
    lower_parts = jnp.transpose(lower[0], (1, 2, 0, 3))
    own_lower, spare_lower = pack(lower_parts, pick(slot, col_index * n_row + row_index), size, False)
    own_lower, spare_lower, upper = fence((own_lower, spare_lower, upper))
    upper_parts = jnp.transpose(upper[0], (1, 2, 0, 3))
    own_upper = pack(upper_parts, pick(slot, row_index * n_col + col_index), size, True)

    def first_part(size):
        def run(own_upper, own_lower, spare_lower):
            sums = row_product(inverse, None, col_index, pole_index, row_slot, weight, own_upper, size, tile, share)
            sums, own_lower = fence((sums, own_lower))
            pieces = [(own_lower, spare_lower)]
            acc, token = column_phase(
                inverse, None, [row_index], [jnp.int32(0)], [], col_slot, weight, pieces, [], size, n_col
            )
            return sums, acc, token

        return run

    given = diag_inverse[0].astype(F32)
    own_term = weight[0] * given[:, 1] + weight[1] * given[:, 0]
    owner = jnp.logical_and(row_index == 0, col_index == 0)
    own_term = jnp.where(owner, own_term, 0.0)

    tile = min(1024, part_cols)
    share = part_cols // (n_row * n_pole)
    passing = hop((own_lower,), "row", n_row, 1)
    upper_got = [p for pair in line_gather(own_upper[0], "col", n_col) for p in pair]
    sums, acc, token = lax.cond(
        crowded, first_part(size), first_part(size.usual()), own_upper, own_lower, spare_lower
    )
    passing, own_upper, upper_got, sums, token, own_term = fence(
        (passing, own_upper, upper_got, sums, token, own_term)
    )

    def send(pieces):
        return jax.tree.leaves([line_gather(pieces[0], "row", n_row), line_gather(pieces[1], "col", n_col)])

    def skip(pieces):
        return list(blank(jax.eval_shape(send, pieces)))

    spread = lax.cond(crowded, send, skip, (spare_lower, own_upper[1]))
    row_spares, col_spares = spread[: len(spread) - len(upper_got)], spread[len(spread) - len(upper_got) :]
    uppers = [own_upper] + list(zip(upper_got, col_spares))

    def second_part(size):
        def run(sums, got, col_spares):
            for source, *pieces in zip(upper_from, got, col_spares):
                sums = row_product(inverse, sums, source, pole_index, row_slot, weight, pieces, size, tile, share)
            if len(sums) == 2:
                terms = (sums[0], swap(sums[1], "pole"))
            else:
                both = jnp.transpose(sums[0], (1, 0, 2)).reshape(supers * width, n_row, n_pole, share)
                both = jnp.transpose(both, (2, 1, 0, 3))
                terms = (pick(both, pole_index), swap(pick(both, 1 - pole_index), "pole"))
            return terms, scatter_codes(terms, (), "row", n_row, 0)

        return run

    held = [(1, passing)]
    if n_row > 2:
        passing = hop(passing, "row", n_row, 2)
    terms, codes = lax.cond(
        crowded, second_part(size), second_part(size.usual()), sums, upper_got, col_spares
    )
    passing, terms, codes = fence((passing, terms, codes))

    def spare_pair(t):
        return row_spares[(t - 1) * len(held[-1][1]) : t * len(held[-1][1])]

    brought = [p for hop_pair in lower_from[1:] for p in hop_pair]
    rank = [jnp.int32(0)]
    for p in brought:
        rank.append(rank[-1] + (p >= 0))

    def nth(j, values):
        found = jnp.int32(0)
        for i, p in enumerate(brought):
            found = jnp.where(jnp.logical_and(p >= 0, rank[i] == j), values[i], found)
        return found

    def phase(acc, held, last):
        pieces = [p for t, pair in held for p in zip(pair, spare_pair(t))]
        taken = [n_row - 2] if last else range(n_row - 2)
        sources = [nth(j, brought) for j in taken]
        which = [nth(j, range(len(brought))) for j in taken]
        if not last:
            return column_phase(inverse, acc, sources, which, [], col_slot, weight, pieces, [], size, n_col)
        positions = [col_index] + upper_from + [pole_index]
        slots = jnp.concatenate([col_slot, row_slot])
        return column_phase(
            inverse, acc, sources, which, positions, slots, weight, pieces, uppers, size, n_col, (own_term,), (token,)
        )

    stage = 0
    carried = ()
    for t in range(3, n_row):
        held.append((t - 1, passing))
        passing = hop(passing, "row", n_row, t)
        carried = scatter_move(codes, "row", n_row, stage)
        stage += 1
        if t == n_row - 1:
            acc, token = phase(acc, held, False)
        codes = scatter_codes(terms, carried, "row", n_row, stage)
        passing, token, terms, codes = fence((passing, token, terms, codes))
    if n_row > 2:
        held.append((n_row - 1, passing))
        carried = scatter_move(codes, "row", n_row, stage)
        stage += 1
    keep, give, t_part = phase(acc, held, True)
    keep, give, t_part, terms, carried, codes = fence((keep, give, t_part, terms, carried, codes))
    if n_row > 2:
        codes = scatter_codes(terms, carried, "row", n_row, stage)

    carried = scatter_move(codes, "row", n_row, stage)
    col_terms = (keep, swap(give, "pole"))
    col_codes = scatter_codes(col_terms, (), "col", n_col, 0)

    t_part = t_part.reshape(n_pole, -1, width)
    t_sum = pick(t_part, pole_index) + swap(pick(t_part, 1 - pole_index), "pole")
    if n_col == 2:
        t_sum = t_sum.reshape(n_col, -1, width)
        t_sum = pick(t_sum, col_index) + swap(pick(t_sum, 1 - col_index), "col")
    else:
        t_sum = direct_sum(t_sum, "col", n_col)
    t_sum, col_codes, carried = fence((t_sum, col_codes, carried))
    for t in range(n_col - 1):
        col_carried = scatter_move(col_codes, "col", n_col, t)
        if t < n_col - 2:
            col_codes = scatter_codes(col_terms, col_carried, "col", n_col, t + 1)
    t_sum = direct_sum(t_sum, "row", n_row)
    row_density = finish(terms, row_index, carried, supers, width, True)
    t_sum, col_carried, row_density = fence((t_sum, col_carried, row_density))
    column_density = finish(col_terms, col_index, col_carried, supers, width, False)
    if n_col == 2:
        t_sum = halves_back(t_sum, "col", n_col)
    t_sum, column_density = fence((t_sum, column_density))
    diagonal_density = halves_back(t_sum, "pole", n_pole).reshape(supers, width, width)
    return (column_density, row_density, diagonal_density)


def solution(mesh):
    return jax.shard_map(
        body,
        mesh=mesh,
        in_specs=(
            P(("groups", "pole"), None, "row", "col"),
            P(("groups", "pole"), ("col", "row"), None, None, None),
            P(("groups", "pole"), ("row", "col"), None, None, None),
            P(("groups", "pole"), None, None, None, None),
            P(("groups", "pole"), None),
            P("groups", None),
        ),
        out_specs=(
            P(("groups", "row", "col", "pole"), None, None),
            P(("groups", "col", "row", "pole"), None, None),
            P("groups", None, None),
        ),
        check_vma=False,
    )
```
